256 devices in a mesh: gx: 32 (over y, z), gy: 8 (over x, core).
Axes of the slice: x: 4, y: 4, z: 8, core: 2. Of those that a mesh axis runs over, the one named last changes fastest.
Arguments:
- right_side: float32 [64, 256, 1024], P(None, 'gx', 'gy'), may hold values from -6 to 6
- conductivity: float32 [64, 256, 1024], P(None, 'gx', 'gy'), may hold values from 0.1 to 10
Outputs:
- pressure: float32 [64, 256, 1024], P(None, 'gx', 'gy')
- residual: float32 [64, 256, 1024], P(None, 'gx', 'gy')
The draws below stay inside these ranges and needn't reach their ends.
All inputs are finite; a program needn't handle non-finite values.
Results may differ from the reference program's by a relative error of at most 0.0003.
Values sent between devices are 32-bit elements; how exact they have to be, the bound alone decides.
No kernel may reach another device: no remote copies, remote signals or barrier semaphores. Data moves between devices by JAX's collectives and lax.ppermute only.
A program may use at most 128 MiB of HBM per device.

```python
import math
import jax
import jax.numpy as jnp

NZ = 64
COARSE = 8
NX = 256
NY = 1024


def draw_right_side(key, part):
    key = jax.random.fold_in(key, 7)
    drawn = jnp.clip(jax.random.normal(key, (NZ, NX, NY), jnp.float32), -6.0, 6.0)
    return drawn


def shard_levels(stream_key, shape, split, least, high):
    gain, own = 1.0, jax.random.fold_in(stream_key, 6)
    for position, parts in split:
        steps = jnp.exp(jax.random.uniform(jax.random.fold_in(own, position), (parts,), jnp.float32, least / len(split), high / len(split)))
        gain = gain * jnp.repeat(steps, shape[position] // parts).reshape([-1 if axis == position else 1 for axis in range(len(shape))])
    return gain


def setup_inputs(seed: int = 0) -> dict:
    key_list = jax.random.split(jax.random.key(seed), 3)
    right_side = draw_right_side(jax.random.fold_in(key_list[2], 71), 0)
    conductivity = jnp.clip(jnp.exp(math.log(10.0) - 4.6051702 * jax.random.uniform(key_list[1], (NZ, NX, NY), jnp.float32) ** shard_levels(key_list[1], (NZ, NX, NY), ((1, 32), (2, 8)), -0.2, 0.2)), 0.1, 10.0)
    return dict(right_side=right_side, conductivity=conductivity)


LOW_BOUND = 0.3
HIGH_BOUND = 2.0
COARSE_LOW = 0.02


def neighbours(padded):
    return [padded[2:, 1:-1, 1:-1], padded[:-2, 1:-1, 1:-1], padded[1:-1, 2:, 1:-1], padded[1:-1, :-2, 1:-1], padded[1:-1, 1:-1, 2:], padded[1:-1, 1:-1, :-2]]


def make_operator(padded_conduct, factor):
    centre = padded_conduct[1:-1, 1:-1, 1:-1]
    weights = [0.5 * (centre + other) for other in neighbours(padded_conduct)]
    diagonal = factor * (weights[0] + weights[1] + weights[2] + weights[3] + weights[4] + weights[5])
    return weights, diagonal, factor


def stencil(field, padded_field, operator):
    weights, diagonal, factor = operator
    others = neighbours(padded_field)
    total = weights[0] * others[0]
    for index in range(1, 6):
        total = total + weights[index] * others[index]
    return diagonal * field - factor * total


def coarsen(field):
    shape = field.shape
    blocks = field.reshape(shape[0] // 2, 2, shape[1] // 2, 2, shape[2] // 2, 2)
    return jnp.mean(blocks, axis=(1, 3, 5))


def refine(field):
    return jnp.repeat(jnp.repeat(jnp.repeat(field, 2, axis=0), 2, axis=1), 2, axis=2)


def smooth(operate, diagonal, source, start, sweeps, lower):
    middle = (HIGH_BOUND + lower) / 2
    half_width = (HIGH_BOUND - lower) / 2
    ratio_mid = middle / half_width
    cheb_rho = 1 / ratio_mid
    residue = source if start is None else source - operate(start)
    update = residue / diagonal / middle
    iterate = update if start is None else start + update
    for sweep in range(sweeps - 1):
        residue = source - operate(iterate)
        rho_next = 1 / (2 * ratio_mid - cheb_rho)
        update = (rho_next * cheb_rho) * update + (2 * rho_next / half_width) * (residue / diagonal)
        iterate = iterate + update
        cheb_rho = rho_next
    return iterate


def reference(right_side, conductivity):
    conducts = [conductivity]
    for grid_level in range(3):
        conducts.append(coarsen(conducts[-1]))
    operators = [make_operator(jnp.pad(conducts[g], 1), 0.25 ** g) for g in range(4)]

    def operate_at(grid_level):
        operator = operators[grid_level]
        return lambda field: stencil(field, jnp.pad(field, 1), operator)

    def vcycle(grid_level, source):
        diagonal = operators[grid_level][1]
        operate = operate_at(grid_level)
        if grid_level == 3:
            return smooth(operate, diagonal, source, None, COARSE, COARSE_LOW)
        iterate = smooth(operate, diagonal, source, None, 2, LOW_BOUND)
        residue = source - operate(iterate)
        iterate = iterate + refine(vcycle(grid_level + 1, coarsen(residue)))
        return smooth(operate, diagonal, source, iterate, 2, LOW_BOUND)

    pressure = vcycle(0, right_side)
    return pressure, right_side - operate_at(0)(pressure)
```

```python
import functools

import jax
import jax.numpy as jnp
from jax import lax
from jax.experimental import pallas as pl
from jax.experimental.pallas import tpu as pltpu
from jax.sharding import PartitionSpec as P

F32 = jnp.float32
COARSE = 8
LOW_BOUND = 0.3
HIGH_BOUND = 2.0
COARSE_LOW = 0.02
VMEM_LIMIT = 48 * 1024 * 1024

KX, BX, KY, BY = 5, 4, 13, 12


def pairs(size, offset):
    found = []
    for i in range(offset, size - 1, 2):
        found += [(i, i + 1), (i + 1, i)]
    return found


def swap(value, axis, offset):
    return lax.ppermute(value, axis, pairs(lax.axis_size(axis), offset))


def chebyshev(sweeps, lower):
    middle = (HIGH_BOUND + lower) / 2
    half_width = (HIGH_BOUND - lower) / 2
    ratio = middle / half_width
    rho = 1 / ratio
    steps = []
    for _ in range(sweeps - 1):
        rho_next = 1 / (2 * ratio - rho)
        steps.append((rho_next * rho, 2 * rho_next / half_width))
        rho = rho_next
    return middle, steps


def iota(shape, axis):
    return lax.broadcasted_iota(jnp.int32, shape, axis)


def dot(a, b):
    return jnp.dot(a, b, preferred_element_type=F32, precision=lax.Precision.HIGHEST)


def coarsen_matrix(fine, coarse, right, left, scale):
    f, c = iota((fine, coarse), 0), iota((fine, coarse), 1)
    ahead = (f < right) & (c == lax.shift_right_logical(f, 1))
    behind = (f >= fine - left) & (coarse - c == lax.shift_right_logical(fine - f + 1, 1))
    return jnp.where(ahead | behind, scale, 0.0).astype(F32)


def refine_matrix(coarse, fine, right, left):
    c, f = iota((coarse, fine), 0), iota((coarse, fine), 1)
    ahead = (f < right) & (c == lax.shift_right_logical(f, 1))
    behind = (f >= fine - left) & (coarse - c == lax.shift_right_logical(fine - f + 1, 1))
    return jnp.where(ahead | behind, 1.0, 0.0).astype(F32)


def turn(value, shift, axis):
    shift = shift % value.shape[axis]
    return value if shift == 0 else pltpu.roll(value, shift, axis=axis)


def weights_row(kc, km, kp, factor):
    half = 0.5 * factor
    axis = kc.ndim - 2
    depth = kc.shape[axis]
    z = iota(kc.shape, axis)
    low, top = z == 0, z == depth - 1
    up = half * (kc + jnp.where(top, 0.0, turn(kc, -1, axis)))
    down = half * (kc + jnp.where(low, 0.0, turn(kc, 1, axis)))
    ahead = half * (kc + turn(kc, -1, axis + 1))
    behind = half * (kc + turn(kc, 1, axis + 1))
    right = half * (kc + kp)
    left = half * (kc + km)
    diagonal = up + down + ahead + behind + right + left
    inverse = jnp.where(kc > 0, 1.0 / diagonal, 0.0)
    up = jnp.where(top, 0.0, up)
    down = jnp.where(low, 0.0, down)
    weights = [w * inverse for w in (left, right, behind, ahead, down, up)]
    return weights, inverse, diagonal


def neighbour_sum(weights, below, centre, above):
    axis = centre.ndim - 2
    left, right, behind, ahead, down, up = weights
    total = left * below + right * above
    total = total + behind * turn(centre, 1, axis + 1) + ahead * turn(centre, -1, axis + 1)
    return total + down * turn(centre, 1, axis) + up * turn(centre, -1, axis)


class Level:
    def __init__(self, k, weights, bh, x, p, factor):
        self.k, self.weights, self.bh, self.x, self.p, self.factor = k, weights, bh, x, p, factor

    def rows(self, low, high, body):
        def step(q, carry):
            body(q)
            return carry

        lax.fori_loop(low, high, step, 0)

    def set_up(self, low, high, b, diagonal=None):
        def body(q):
            weights, inverse, diag = weights_row(self.k[q], self.k[q - 1], self.k[q + 1], self.factor)
            for n in range(6):
                self.weights[n, q] = weights[n]
            self.bh[q] = b[q] * inverse
            if diagonal is not None:
                diagonal[q] = diag

        self.rows(low, high, body)

    def total(self, x, q):
        return neighbour_sum([self.weights[n, q] for n in range(6)], x[q - 1], x[q], x[q + 1])

    def pre(self, low, high):
        middle, ((c1, c2),) = chebyshev(2, LOW_BOUND)

        def body(q):
            first = self.bh[q]
            self.x[q] = (1 / middle) * (1 + c1 - c2 + c2 * middle) * first + (c2 / middle) * self.total(self.bh, q)

        self.rows(low, high, body)

    def post(self, low, high, out):
        middle, ((c1, c2),) = chebyshev(2, LOW_BOUND)

        def first(q):
            update = (self.bh[q] - self.x[q] + self.total(self.x, q)) * (1 / middle)
            self.p[q] = update
            out[q] = self.x[q] + update

        def second(q):
            residue = self.bh[q] - out[q] + self.total(out, q)
            self.x[q] = out[q] + c1 * self.p[q] + c2 * residue

        self.rows(low - 1, high + 1, first)
        self.rows(low, high, second)


def spec(n):
    return [pl.BlockSpec(memory_space=pltpu.VMEM)] * n


def call(body, outs, scratch, *args):
    return pl.pallas_call(
        body,
        out_shape=[jax.ShapeDtypeStruct(s, F32) for s in outs],
        in_specs=spec(len(args)),
        out_specs=spec(len(outs)),
        scratch_shapes=[pltpu.VMEM(s, F32) for s in scratch],
        compiler_params=pltpu.CompilerParams(vmem_limit_bytes=VMEM_LIMIT),
    )(*args)


def odd(axis):
    return lax.rem(lax.axis_index(axis), 2) == 1


def pack_kernel(b_ref, k_ref, ya, yb, xa, xb):
    odd_x, odd_y = odd("gx"), odd("gy")
    lane = iota((64, 128), 1)
    for n, (ref, width) in enumerate(((k_ref, KY), (b_ref, BY))):
        first, last = jnp.zeros((64, 128), F32), jnp.zeros((64, 128), F32)
        for i in range(8):
            plane = ref[pl.ds(i, 64, stride=8), :]
            here = (lane >= 16 * i) & (lane < 16 * i + width)
            first = jnp.where(here, turn(plane, 16 * i, 1), first)
            last = jnp.where(here, turn(plane, 16 * i + width, 1), last)
        ya[n] = jnp.where(odd_y, first, last)
        yb[n] = jnp.where(odd_y, last, first)
    at = 0
    for ref, width in ((k_ref, KX), (b_ref, BX)):
        for i in range(width):
            first = ref[pl.ds(i, 64, stride=8), :]
            last = ref[pl.ds(8 - width + i, 64, stride=8), :]
            xa[at] = jnp.where(odd_x, first, last)
            xb[at] = jnp.where(odd_x, last, first)
            at += 1


def assemble(strips, n, width, i, lane):
    left, right = strips
    right_part = turn(right[n], -16 * i, 1)
    left_part = turn(left[n], 128 - width - 16 * i, 1)
    return jnp.where(lane < width, right_part, jnp.where(lane >= 128 - width, left_part, 0.0))


def first_kernel(b_ref, k_ref, xa, xb, ya, yb, k_out, b_out, x_out, k1_out, b1_out, sa, sb, weights, bh, diagonal, wide, thin):
    odd_x, odd_y = odd("gx"), odd("gy")
    lane = iota((64, 128), 1)

    def by_y(a, b):
        return jnp.where(odd_y, a, b), jnp.where(odd_y, b, a)

    def fill(out, n, q, plane, strips, i, width):
        out[q, :, 0:128] = plane
        out[q, :, 128:256] = assemble(strips, n, width, i, lane)

    own = [by_y(ya[n], yb[n]) for n in range(2)]
    own = ([own[0][0], own[1][0]], [own[0][1], own[1][1]])
    for i in range(8):
        fill(k_out, 0, i + 5, k_ref[pl.ds(i, 64, stride=8), :], own, i, KY)
        fill(b_out, 1, i + 5, b_ref[pl.ds(i, 64, stride=8), :], own, i, BY)
    for side in range(2):

        def pick(n):
            a, b = xa[n], xb[n]
            return jnp.where(odd_x, a, b) if side == 0 else jnp.where(odd_x, b, a)

        strips = [by_y(pick(9 + n), pick(11 + n)) for n in range(2)]
        strips = ([strips[0][0], strips[1][0]], [strips[0][1], strips[1][1]])
        for j in range(KX):
            fill(k_out, 0, j if side == 0 else 13 + j, pick(j), strips, 3 + j if side == 0 else j, KY)
        for j in range(BX):
            fill(b_out, 1, 1 + j if side == 0 else 13 + j, pick(KX + j), strips, 4 + j if side == 0 else j, BY)

    level = Level(k_out, weights, bh, x_out, None, 1.0)
    level.set_up(1, 17, b_out, diagonal)
    level.pre(2, 16)

    def residue(q):
        return diagonal[q] * (bh[q] - x_out[q] + level.total(x_out, q))

    def pair(m, carry):
        wide[m] = residue(2 * m + 3) + residue(2 * m + 4)
        return carry

    lax.fori_loop(0, 6, pair, 0)
    for m in range(8):
        wide[6 + m] = k_out[2 * m + 1] + k_out[2 * m + 2]
    matrix = coarsen_matrix(256, 128, 140, 12, 0.125)
    flat = dot(wide[...].reshape(14 * 64, 256), matrix)
    thin[...] = flat
    done = []
    for m in range(14):
        done.append(thin[pl.ds(64 * m, 32, stride=2), :] + thin[pl.ds(64 * m + 1, 32, stride=2), :])
    for m in range(6):
        b1_out[m] = done[m]
    for m in range(8):
        k1_out[m] = done[6 + m]
    for m in range(5):
        sa[m] = jnp.where(odd_x, done[m + 1], done[m])
        sb[m] = jnp.where(odd_x, done[m], done[m + 1])
    for m in range(6):
        sa[5 + m] = jnp.where(odd_x, done[8 + m], done[6 + m])
        sb[5 + m] = jnp.where(odd_x, done[6 + m], done[8 + m])


def second_kernel(count, b1, k1, ra, rb, k_out, b_out, x_out, g_out, weights, bh, diagonal, thin):
    odd_x = odd("gx")
    for side in range(2):

        def pick(n):
            a, b = ra[n], rb[n]
            return jnp.where(odd_x, a, b) if side == 0 else jnp.where(odd_x, b, a)

        for j in range(6):
            k_out[j if side == 0 else 10 + j] = pick(5 + j)
        for j in range(5):
            b_out[1 + j if side == 0 else 10 + j] = pick(j)
    for j in range(4):
        k_out[6 + j] = k1[2 + j]
        b_out[6 + j] = b1[1 + j]

    level = Level(k_out, weights, bh, x_out, None, 0.25)
    level.set_up(1, 15, b_out, diagonal)
    level.pre(2, 14)

    def residue(q):
        return diagonal[q] * (bh[q] - x_out[q] + level.total(x_out, q))

    parts = [residue(6) + residue(7), residue(8) + residue(9), k_out[6] + k_out[7], k_out[8] + k_out[9]]
    matrix = coarsen_matrix(128, 128, 64, 0, 0.125)
    thin[...] = dot(jnp.concatenate(parts, axis=0), matrix)
    payload = jnp.zeros((16, 128), F32)
    for n in range(4):
        part = thin[pl.ds(32 * n, 16, stride=2), :] + thin[pl.ds(32 * n + 1, 16, stride=2), :]
        payload = payload + turn(part, 32 * n, 1)
    for n in range(count):
        g_out[n] = payload


def last_kernel(
    count, g, ga, gb, k1, b1, x1_in, k0, b0, x0_in, pressure, residual,
    k2, b2, w2, bh2, x2, y2, p2, fine2, coarse2, w1, bh1, x1, y1, p1, stack1, w0, bh0, d0, x0, y0, p0, stack0,
):
    odd_y = odd("gy")
    me = lax.axis_index("gx")
    lane = iota((16, 128), 1)

    def window(j, carry):
        device = me - 11 + j
        inside = (device >= 0) & (device < count)
        at = jnp.clip(device, 0, count - 1)
        own, a, b = g[at], ga[at], gb[at]
        left, right = jnp.where(odd_y, a, b), jnp.where(odd_y, b, a)
        for n, out in ((0, b2), (2, k2)):
            for m in range(2):
                s = -32 * (n + m)
                value = jnp.where(lane < 32, turn(own, s, 1), jnp.where(lane < 64, turn(right, s + 32, 1), jnp.where(lane >= 96, turn(left, s + 96, 1), 0.0)))
                out[2 * j + m] = jnp.where(inside, value, 0.0)
        return carry

    lax.fori_loop(0, 23, window, 0)
    level = Level(k2, w2, bh2, x2, p2, 0.0625)
    level.set_up(1, 45, b2, y2)
    level.pre(2, 44)

    def residue(q):
        return y2[q] * (bh2[q] - x2[q] + level.total(x2, q))

    def pair(m, carry):
        fine2[m] = residue(2 * m) + residue(2 * m + 1)
        return carry

    lax.fori_loop(2, 21, pair, 0)
    zero = jnp.zeros((16, 128), F32)
    for m in (0, 1, 21, 22):
        fine2[m] = zero
    for m in range(23):
        fine2[23 + m] = k2[2 * m] + k2[2 * m + 1]
    coarse2[...] = dot(fine2[...].reshape(46 * 16, 128), coarsen_matrix(128, 128, 64, 32, 0.125))
    both = coarse2[pl.ds(0, 46 * 8, stride=2), :] + coarse2[pl.ds(1, 46 * 8, stride=2), :]
    both = both.reshape(46, 8, 128)
    b3, k3 = both[:23], both[23:]
    none = jnp.zeros((1, 8, 128), F32)

    def after(value):
        return jnp.concatenate([value[1:], none], axis=0)

    def before(value):
        return jnp.concatenate([none, value[:-1]], axis=0)

    w3, inverse, _ = weights_row(k3, before(k3), after(k3), 0.015625)
    middle, steps = chebyshev(COARSE, COARSE_LOW)
    source = b3 * inverse
    update = source * (1 / middle)
    e3 = update
    for c1, c2 in steps:
        update = c1 * update + c2 * (source - e3 + neighbour_sum(w3, before(e3), e3, after(e3)))
        e3 = e3 + update

    tall = coarse2
    for m in range(5):
        for half in range(2):
            tall[pl.ds(16 * m + half, 8, stride=2), :] = e3[9 + m]
    fine = dot(tall[0 : 5 * 16, :], refine_matrix(128, 128, 64, 32))
    for m in range(10):
        part = fine[16 * (m // 2) : 16 * (m // 2) + 16]
        x2[18 + m] = x2[18 + m] + part
    level.post(20, 26, y2)

    for m in range(6):
        for half in range(2):
            stack1[pl.ds(32 * m + half, 16, stride=2), :] = x2[20 + m]
    fine = dot(stack1[...], refine_matrix(128, 128, 70, 6))
    for m in range(12):
        x1[2 + m] = x1_in[2 + m] + fine[32 * (m // 2) : 32 * (m // 2) + 32]
    level = Level(k1, w1, bh1, x1, p1, 0.25)
    level.set_up(3, 13, b1)
    level.post(4, 12, y1)

    for m in range(8):
        for half in range(2):
            stack0[pl.ds(64 * m + half, 32, stride=2), :] = x1[4 + m]
    matrix = refine_matrix(128, 256, 140, 12)
    fine = dot(stack0[...], matrix)
    for m in range(14):
        row = (m + 1) // 2
        x0[2 + m] = x0_in[2 + m] + fine[64 * row : 64 * row + 64]
    level = Level(k0, w0, bh0, x0, p0, 1.0)
    level.set_up(3, 15, b0, d0)
    level.post(4, 14, y0)
    for i in range(8):
        q = 5 + i
        value = x0[q]
        left = d0[q] * (bh0[q] - value + level.total(x0, q))
        pressure[pl.ds(i, 64, stride=8), :] = value[:, 0:128]
        residual[pl.ds(i, 64, stride=8), :] = left[:, 0:128]


def on_device(right_side, conductivity):
    count = lax.axis_size("gx")
    b, k = right_side.reshape(512, 128), conductivity.reshape(512, 128)
    ya, yb, xa, xb = call(pack_kernel, [(2, 64, 128)] * 2 + [(13, 64, 128)] * 2, [], b, k)
    ya, yb = swap(ya, "gy", 0), swap(yb, "gy", 1)

    def with_y(strip):
        strip = lax.dynamic_update_slice(strip, ya, (9, 0, 0))
        return lax.dynamic_update_slice(strip, yb, (11, 0, 0))

    xa, xb = swap(with_y(xa), "gx", 0), swap(with_y(xb), "gx", 1)
    rows0, rows1 = (18, 64, 256), (16, 32, 128)
    k0, b0, x0, k1, b1, sa, sb = call(
        first_kernel,
        [rows0, rows0, rows0, (8, 32, 128), (6, 32, 128), (11, 32, 128), (11, 32, 128)],
        [(6,) + rows0, rows0, rows0, (14, 64, 256), (14 * 64, 128)],
        b, k, xa, xb, ya, yb,
    )
    ra, rb = swap(sa, "gx", 0), swap(sb, "gx", 1)
    k1, b1, x1, g = call(
        functools.partial(second_kernel, count),
        [rows1, rows1, rows1, (count, 16, 128)],
        [(6,) + rows1, rows1, rows1, (128, 128)],
        b1, k1, ra, rb,
    )
    g = lax.all_to_all(g, "gx", 0, 0, tiled=True)
    ga, gb = swap(g, "gy", 0), swap(g, "gy", 1)
    rows2 = (46, 16, 128)
    pressure, residual = call(
        functools.partial(last_kernel, count),
        [(512, 128)] * 2,
        [rows2, rows2, (6,) + rows2, rows2, rows2, rows2, rows2, (46, 16, 128), (46 * 16, 128)]
        + [(6,) + rows1, rows1, rows1, rows1, rows1, (6 * 32, 128)]
        + [(6,) + rows0, rows0, rows0, rows0, rows0, rows0, (8 * 64, 128)],
        g, ga, gb, k1, b1, x1, k0, b0, x0,
    )
    return pressure.reshape(64, 8, 128), residual.reshape(64, 8, 128)


def solution(mesh):
    place = P(None, "gx", "gy")
    return jax.shard_map(
        on_device, mesh=mesh, in_specs=(place, place), out_specs=(place, place), check_vma=False
    )
```

```python
import functools

import jax
import jax.numpy as jnp
from jax import lax
from jax.experimental import pallas as pl
from jax.experimental.pallas import tpu as pltpu
from jax.sharding import PartitionSpec as P

F32 = jnp.float32
COARSE = 8
LOW_BOUND = 0.3
HIGH_BOUND = 2.0
COARSE_LOW = 0.02
VMEM_LIMIT = 28 * 1024 * 1024

SHAPE0, SHAPE1, SHAPE2, WINDOW_UNROLL = (1,True), (4, True), (8, True), True

KX, BX, KY, BY = 5, 4, 13, 12


def pairs(size, offset):
    found = []
    for i in range(offset, size - 1, 2):
        found += [(i, i + 1), (i + 1, i)]
    return found


def swap(value, axis, offset):
    return lax.ppermute(value, axis, pairs(lax.axis_size(axis), offset))


def chebyshev(sweeps, lower):
    middle = (HIGH_BOUND + lower) / 2
    half_width = (HIGH_BOUND - lower) / 2
    ratio = middle / half_width
    rho = 1 / ratio
    steps = []
    for _ in range(sweeps - 1):
        rho_next = 1 / (2 * ratio - rho)
        steps.append((rho_next * rho, 2 * rho_next / half_width))
        rho = rho_next
    return middle, steps


def iota(shape, axis):
    return lax.broadcasted_iota(jnp.int32, shape, axis)


def dot(a, b):
    b = b.astype(jnp.bfloat16)
    total = None
    for _ in range(3):
        piece = a.astype(jnp.bfloat16)
        a = a - piece.astype(F32)
        part = jnp.dot(piece, b, preferred_element_type=F32)
        total = part if total is None else total + part
    return total


def coarsen_matrix(fine, coarse, right, left, scale):
    f, c = iota((fine, coarse), 0), iota((fine, coarse), 1)
    ahead = (f < right) & (c == lax.shift_right_logical(f, 1))
    behind = (f >= fine - left) & (coarse - c == lax.shift_right_logical(fine - f + 1, 1))
    return jnp.where(ahead | behind, scale, 0.0).astype(F32)


def refine_matrix(coarse, fine, right, left):
    c, f = iota((coarse, fine), 0), iota((coarse, fine), 1)
    ahead = (f < right) & (c == lax.shift_right_logical(f, 1))
    behind = (f >= fine - left) & (coarse - c == lax.shift_right_logical(fine - f + 1, 1))
    return jnp.where(ahead | behind, 1.0, 0.0).astype(F32)


def turn(value, shift, axis):
    shift = shift % value.shape[axis]
    return value if shift == 0 else pltpu.roll(value, shift, axis=axis)


def weights_row(kc, km, kp, factor):
    half = 0.5 * factor
    axis = kc.ndim - 2
    depth = kc.shape[axis]
    z = iota(kc.shape, axis)
    low, top = z == 0, z == depth - 1
    up = half * (kc + jnp.where(top, 0.0, turn(kc, -1, axis)))
    down = half * (kc + jnp.where(low, 0.0, turn(kc, 1, axis)))
    ahead = half * (kc + turn(kc, -1, axis + 1))
    behind = half * (kc + turn(kc, 1, axis + 1))
    right = half * (kc + kp)
    left = half * (kc + km)
    diagonal = up + down + ahead + behind + right + left
    inverse = jnp.where(kc > 0, 1.0 / diagonal, 0.0)
    up = jnp.where(top, 0.0, up)
    down = jnp.where(low, 0.0, down)
    weights = [w * inverse for w in (left, right, behind, ahead, down, up)]
    return weights, inverse, diagonal


def neighbour_sum(weights, below, centre, above):
    axis = centre.ndim - 2
    left, right, behind, ahead, down, up = weights
    total = left * below + right * above
    total = total + behind * turn(centre, 1, axis + 1) + ahead * turn(centre, -1, axis + 1)
    return total + down * turn(centre, 1, axis) + up * turn(centre, -1, axis)


def rows(low, high, body, chunk, unroll):
    full = (high - low) // chunk

    def step(n, carry):
        body(pl.ds(low + n * chunk, chunk), pl.ds(low + n * chunk - 1, chunk), pl.ds(low + n * chunk + 1, chunk))
        return carry

    lax.fori_loop(0, full, step, 0, unroll=unroll)
    at = low + full * chunk
    if at < high:
        body(pl.ds(at, high - at), pl.ds(at - 1, high - at), pl.ds(at + 1, high - at))


class Level:
    def __init__(self, k, weights, bh, x, p, factor, chunk, unroll):
        self.k, self.weights, self.bh, self.x, self.p, self.factor = k, weights, bh, x, p, factor
        self.chunk, self.unroll = chunk, unroll

    def rows(self, low, high, body):
        rows(low, high, body, self.chunk, self.unroll)

    def set_up(self, low, high, b, diagonal):
        def body(q, below, above):
            weights, inverse, diag = weights_row(self.k[q], self.k[below], self.k[above], self.factor)
            for n in range(6):
                self.weights[n, q] = weights[n]
            self.bh[q] = b[q] * inverse
            diagonal[q] = diag

        self.rows(low, high, body)

    def total(self, x, q, below, above):
        return neighbour_sum([self.weights[n, q] for n in range(6)], x[below], x[q], x[above])

    def pre(self, low, high):
        middle, ((c1, c2),) = chebyshev(2, LOW_BOUND)

        def body(q, below, above):
            first = self.bh[q]
            total = self.total(self.bh, q, below, above)
            self.x[q] = (1 / middle) * (1 + c1 - c2 + c2 * middle) * first + (c2 / middle) * total

        self.rows(low, high, body)

    def residue(self, low, high, diagonal, out, at):
        def body(q, below, above):
            value = diagonal[q] * (self.bh[q] - self.x[q] + self.total(self.x, q, below, above))
            out[pl.ds(q.start + (at - low), q.size)] = value

        self.rows(low, high, body)

    def post(self, low, high, out):
        middle, ((c1, c2),) = chebyshev(2, LOW_BOUND)

        def first(q, below, above):
            update = (self.bh[q] - self.x[q] + self.total(self.x, q, below, above)) * (1 / middle)
            self.p[q] = update
            out[q] = self.x[q] + update

        def second(q, below, above):
            residue = self.bh[q] - out[q] + self.total(out, q, below, above)
            self.x[q] = out[q] + c1 * self.p[q] + c2 * residue

        self.rows(low - 1, high + 1, first)
        self.rows(low, high, second)


def spec(n):
    return [pl.BlockSpec(memory_space=pltpu.VMEM)] * n


def call(body, outs, scratch, *args):
    return pl.pallas_call(
        body,
        out_shape=[jax.ShapeDtypeStruct(s, F32) for s in outs],
        in_specs=spec(len(args)),
        out_specs=spec(len(outs)),
        scratch_shapes=[pltpu.VMEM(s, F32) for s in scratch],
        compiler_params=pltpu.CompilerParams(vmem_limit_bytes=VMEM_LIMIT),
    )(*args)


def odd(axis):
    return lax.rem(lax.axis_index(axis), 2) == 1


def pack_kernel(b_ref, k_ref, ya, yb, xa, xb):
    odd_x, odd_y = odd("gx"), odd("gy")
    lane = iota((64, 128), 1)
    for n, (ref, width) in enumerate(((k_ref, KY), (b_ref, BY))):
        first, last = jnp.zeros((64, 128), F32), jnp.zeros((64, 128), F32)
        for i in range(8):
            plane = ref[pl.ds(i, 64, stride=8), :]
            here = (lane >= 16 * i) & (lane < 16 * i + width)
            first = jnp.where(here, turn(plane, 16 * i, 1), first)
            last = jnp.where(here, turn(plane, 16 * i + width, 1), last)
        ya[n] = jnp.where(odd_y, first, last)
        yb[n] = jnp.where(odd_y, last, first)
    at = 0
    for ref, width in ((k_ref, KX), (b_ref, BX)):
        for i in range(width):
            first = ref[pl.ds(i, 64, stride=8), :]
            last = ref[pl.ds(8 - width + i, 64, stride=8), :]
            xa[at] = jnp.where(odd_x, first, last)
            xb[at] = jnp.where(odd_x, last, first)
            at += 1


def assemble(strips, n, width, i, lane):
    left, right = strips
    right_part = turn(right[n], -16 * i, 1)
    left_part = turn(left[n], 128 - width - 16 * i, 1)
    return jnp.where(lane < width, right_part, jnp.where(lane >= 128 - width, left_part, 0.0))


def first_kernel(b_ref, k_ref, xa, xb, ya, yb, weights, bh, diagonal, x_out, k1_out, b1_out, sa, sb, k_out, b_out, fine, wide, thin):
    odd_x, odd_y = odd("gx"), odd("gy")
    lane = iota((64, 128), 1)

    def by_y(a, b):
        return jnp.where(odd_y, a, b), jnp.where(odd_y, b, a)

    def fill(out, n, q, plane, strips, i, width):
        out[q, :, 0:128] = plane
        out[q, :, 128:256] = assemble(strips, n, width, i, lane)

    own = [by_y(ya[n], yb[n]) for n in range(2)]
    own = ([own[0][0], own[1][0]], [own[0][1], own[1][1]])
    for i in range(8):
        fill(k_out, 0, i + 5, k_ref[pl.ds(i, 64, stride=8), :], own, i, KY)
        fill(b_out, 1, i + 5, b_ref[pl.ds(i, 64, stride=8), :], own, i, BY)
    for side in range(2):

        def pick(n):
            a, b = xa[n], xb[n]
            return jnp.where(odd_x, a, b) if side == 0 else jnp.where(odd_x, b, a)

        strips = [by_y(pick(9 + n), pick(11 + n)) for n in range(2)]
        strips = ([strips[0][0], strips[1][0]], [strips[0][1], strips[1][1]])
        for j in range(KX):
            fill(k_out, 0, j if side == 0 else 13 + j, pick(j), strips, 3 + j if side == 0 else j, KY)
        for j in range(BX):
            fill(b_out, 1, 1 + j if side == 0 else 13 + j, pick(KX + j), strips, 4 + j if side == 0 else j, BY)

    level = Level(k_out, weights, bh, x_out, None, 1.0, *SHAPE0)
    level.set_up(1, 17, b_out, diagonal)
    level.pre(2, 16)
    level.residue(3, 15, diagonal, fine, 0)
    for m in range(6):
        wide[m] = fine[2 * m] + fine[2 * m + 1]
    for m in range(8):
        wide[6 + m] = k_out[2 * m + 1] + k_out[2 * m + 2]
    matrix = coarsen_matrix(256, 128, 140, 12, 0.125)
    flat = dot(wide[...].reshape(14 * 64, 256), matrix)
    thin[...] = flat
    done = []
    for m in range(14):
        done.append(thin[pl.ds(64 * m, 32, stride=2), :] + thin[pl.ds(64 * m + 1, 32, stride=2), :])
    for m in range(6):
        b1_out[m] = done[m]
    for m in range(8):
        k1_out[m] = done[6 + m]
    for m in range(5):
        sa[m] = jnp.where(odd_x, done[m + 1], done[m])
        sb[m] = jnp.where(odd_x, done[m], done[m + 1])
    for m in range(6):
        sa[5 + m] = jnp.where(odd_x, done[8 + m], done[6 + m])
        sb[5 + m] = jnp.where(odd_x, done[6 + m], done[8 + m])


def second_kernel(count, b1, k1, ra, rb, weights, bh, x_out, g_out, k_out, b_out, diagonal, fine, thin):
    odd_x = odd("gx")
    for side in range(2):

        def pick(n):
            a, b = ra[n], rb[n]
            return jnp.where(odd_x, a, b) if side == 0 else jnp.where(odd_x, b, a)

        for j in range(6):
            k_out[j if side == 0 else 10 + j] = pick(5 + j)
        for j in range(5):
            b_out[1 + j if side == 0 else 10 + j] = pick(j)
    for j in range(4):
        k_out[6 + j] = k1[2 + j]
        b_out[6 + j] = b1[1 + j]

    level = Level(k_out, weights, bh, x_out, None, 0.25, *SHAPE1)
    level.set_up(1, 15, b_out, diagonal)
    level.pre(2, 14)
    level.residue(6, 10, diagonal, fine, 0)
    parts = [fine[0] + fine[1], fine[2] + fine[3], k_out[6] + k_out[7], k_out[8] + k_out[9]]
    matrix = coarsen_matrix(128, 128, 64, 0, 0.125)
    thin[...] = dot(jnp.concatenate(parts, axis=0), matrix)
    payload = jnp.zeros((16, 128), F32)
    for n in range(4):
        part = thin[pl.ds(32 * n, 16, stride=2), :] + thin[pl.ds(32 * n + 1, 16, stride=2), :]
        payload = payload + turn(part, 32 * n, 1)
    for n in range(count):
        g_out[n] = payload


def last_kernel(
    count, g, ga, gb, w1, bh1, x1, w0, bh0, d0, x0, pressure, residual,
    k2, b2, w2, bh2, x2, y2, p2, fine2, sums2, coarse2, t1, y1, p1, stack1, t0, y0, p0, stack0,
):
    odd_y = odd("gy")
    me = lax.axis_index("gx")
    lane = iota((16, 128), 1)

    def window(j, carry):
        device = me - 11 + j
        inside = (device >= 0) & (device < count)
        at = jnp.clip(device, 0, count - 1)
        own, a, b = g[at], ga[at], gb[at]
        left, right = jnp.where(odd_y, a, b), jnp.where(odd_y, b, a)
        for n, out in ((0, b2), (2, k2)):
            for m in range(2):
                s = -32 * (n + m)
                value = jnp.where(lane < 32, turn(own, s, 1), jnp.where(lane < 64, turn(right, s + 32, 1), jnp.where(lane >= 96, turn(left, s + 96, 1), 0.0)))
                out[2 * j + m] = jnp.where(inside, value, 0.0)
        return carry

    lax.fori_loop(0, 23, window, 0, unroll=WINDOW_UNROLL)
    level = Level(k2, w2, bh2, x2, p2, 0.0625, *SHAPE2)
    level.set_up(1, 45, b2, y2)
    level.pre(2, 44)
    level.residue(4, 42, y2, fine2, 4)
    zero = jnp.zeros((16, 128), F32)
    for m in (0, 1, 21, 22):
        sums2[m] = zero
    for m in range(2, 21):
        sums2[m] = fine2[2 * m] + fine2[2 * m + 1]
    for m in range(23):
        sums2[23 + m] = k2[2 * m] + k2[2 * m + 1]
    coarse2[...] = dot(sums2[...].reshape(46 * 16, 128), coarsen_matrix(128, 128, 64, 32, 0.125))
    both = coarse2[pl.ds(0, 46 * 8, stride=2), :] + coarse2[pl.ds(1, 46 * 8, stride=2), :]
    both = both.reshape(46, 8, 128)
    b3, k3 = both[:23], both[23:]
    none = jnp.zeros((1, 8, 128), F32)

    def after(value):
        return jnp.concatenate([value[1:], none], axis=0)

    def before(value):
        return jnp.concatenate([none, value[:-1]], axis=0)

    w3, inverse, _ = weights_row(k3, before(k3), after(k3), 0.015625)
    middle, steps = chebyshev(COARSE, COARSE_LOW)
    source = b3 * inverse
    update = source * (1 / middle)
    e3 = update
    for c1, c2 in steps:
        update = c1 * update + c2 * (source - e3 + neighbour_sum(w3, before(e3), e3, after(e3)))
        e3 = e3 + update

    tall = coarse2
    for m in range(5):
        for half in range(2):
            tall[pl.ds(16 * m + half, 8, stride=2), :] = e3[9 + m]
    fine = dot(tall[0 : 5 * 16, :], refine_matrix(128, 128, 64, 32))
    for m in range(10):
        part = fine[16 * (m // 2) : 16 * (m // 2) + 16]
        x2[18 + m] = x2[18 + m] + part
    level.post(20, 26, y2)

    for m in range(6):
        for half in range(2):
            stack1[pl.ds(32 * m + half, 16, stride=2), :] = x2[20 + m]
    fine = dot(stack1[...], refine_matrix(128, 128, 70, 6))
    for m in range(12):
        t1[2 + m] = x1[2 + m] + fine[32 * (m // 2) : 32 * (m // 2) + 32]
    level = Level(None, w1, bh1, t1, p1, 0.25, *SHAPE1)
    level.post(4, 12, y1)

    for m in range(8):
        for half in range(2):
            stack0[pl.ds(64 * m + half, 32, stride=2), :] = t1[4 + m]
    matrix = refine_matrix(128, 256, 140, 12)
    fine = dot(stack0[...], matrix)
    for m in range(14):
        row = (m + 1) // 2
        t0[2 + m] = x0[2 + m] + fine[64 * row : 64 * row + 64]
    level = Level(None, w0, bh0, t0, p0, 1.0, *SHAPE0)
    level.post(4, 14, y0)
    for i in range(8):
        q = 5 + i
        value = t0[q]
        left = d0[q] * (bh0[q] - value + level.total(t0, q, q - 1, q + 1))
        pressure[pl.ds(i, 64, stride=8), :] = value[:, 0:128]
        residual[pl.ds(i, 64, stride=8), :] = left[:, 0:128]


def on_device(right_side, conductivity):
    count = lax.axis_size("gx")
    b, k = right_side.reshape(512, 128), conductivity.reshape(512, 128)
    ya, yb, xa, xb = call(pack_kernel, [(2, 64, 128)] * 2 + [(13, 64, 128)] * 2, [], b, k)
    ya, yb = swap(ya, "gy", 0), swap(yb, "gy", 1)

    def with_y(strip):
        strip = lax.dynamic_update_slice(strip, ya, (9, 0, 0))
        return lax.dynamic_update_slice(strip, yb, (11, 0, 0))

    xa, xb = swap(with_y(xa), "gx", 0), swap(with_y(xb), "gx", 1)
    rows0, rows1 = (18, 64, 256), (16, 32, 128)
    w0, bh0, d0, x0, k1, b1, sa, sb = call(
        first_kernel,
        [(6,) + rows0, rows0, rows0, rows0, (8, 32, 128), (6, 32, 128), (11, 32, 128), (11, 32, 128)],
        [rows0, rows0, (12, 64, 256), (14, 64, 256), (14 * 64, 128)],
        b, k, xa, xb, ya, yb,
    )
    ra, rb = swap(sa, "gx", 0), swap(sb, "gx", 1)
    w1, bh1, x1, g = call(
        functools.partial(second_kernel, count),
        [(6,) + rows1, rows1, rows1, (count, 16, 128)],
        [rows1, rows1, rows1, (4, 32, 128), (128, 128)],
        b1, k1, ra, rb,
    )
    g = lax.all_to_all(g, "gx", 0, 0, tiled=True)
    ga, gb = swap(g, "gy", 0), swap(g, "gy", 1)
    rows2 = (46, 16, 128)
    pressure, residual = call(
        functools.partial(last_kernel, count),
        [(512, 128)] * 2,
        [rows2, rows2, (6,) + rows2, rows2, rows2, rows2, rows2, rows2, rows2, (46 * 16, 128)]
        + [rows1, rows1, rows1, (6 * 32, 128)]
        + [rows0, rows0, rows0, (8 * 64, 128)],
        g, ga, gb, w1, bh1, x1, w0, bh0, d0, x0,
    )
    return pressure.reshape(64, 8, 128), residual.reshape(64, 8, 128)


def solution(mesh):
    place = P(None, "gx", "gy")
    return jax.shard_map(
        on_device, mesh=mesh, in_specs=(place, place), out_specs=(place, place), check_vma=False
    )
```

```python
import functools

import jax
import jax.numpy as jnp
from jax import lax
from jax.experimental import pallas as pl
from jax.experimental.pallas import tpu as pltpu
from jax.sharding import PartitionSpec as P

F32 = jnp.float32
COARSE = 8
LOW_BOUND = 0.3
HIGH_BOUND = 2.0
COARSE_LOW = 0.02
VMEM_LIMIT = 28 * 1024 * 1024

SHAPE0, SHAPE1, SHAPE2, WINDOW_UNROLL = (1,True), (4, True), (8, True), True

PIECES = 4

KX, BX, KY, BY = 7, 6, 13, 12
PACKED = ((0, 0, 9, 14), (0, 9, 9, 14), (0, 18, 4, 14), (1, 0, 10, 12), (1, 10, 10, 12))


def pairs(size, offset):
    found = []
    for i in range(offset, size - 1, 2):
        found += [(i, i + 1), (i + 1, i)]
    return found


def swap(value, axis, offset):
    return lax.ppermute(value, axis, pairs(lax.axis_size(axis), offset))


def chebyshev(sweeps, lower):
    middle = (HIGH_BOUND + lower) / 2
    half_width = (HIGH_BOUND - lower) / 2
    ratio = middle / half_width
    rho = 1 / ratio
    steps = []
    for _ in range(sweeps - 1):
        rho_next = 1 / (2 * ratio - rho)
        steps.append((rho_next * rho, 2 * rho_next / half_width))
        rho = rho_next
    return middle, steps


def iota(shape, axis):
    return lax.broadcasted_iota(jnp.int32, shape, axis)


def dot(a, b):
    b = b.astype(jnp.bfloat16)
    total = None
    for _ in range(3):
        piece = a.astype(jnp.bfloat16)
        a = a - piece.astype(F32)
        part = jnp.dot(piece, b, preferred_element_type=F32)
        total = part if total is None else total + part
    return total


def coarsen_matrix(fine, coarse, right, left, scale):
    f, c = iota((fine, coarse), 0), iota((fine, coarse), 1)
    ahead = (f < right) & (c == lax.shift_right_logical(f, 1))
    behind = (f >= fine - left) & (coarse - c == lax.shift_right_logical(fine - f + 1, 1))
    return jnp.where(ahead | behind, scale, 0.0).astype(F32)


def refine_matrix(coarse, fine, right, left):
    c, f = iota((coarse, fine), 0), iota((coarse, fine), 1)
    ahead = (f < right) & (c == lax.shift_right_logical(f, 1))
    behind = (f >= fine - left) & (coarse - c == lax.shift_right_logical(fine - f + 1, 1))
    return jnp.where(ahead | behind, 1.0, 0.0).astype(F32)


def turn(value, shift, axis):
    shift = shift % value.shape[axis]
    return value if shift == 0 else pltpu.roll(value, shift, axis=axis)


def weights_row(kc, km, kp, factor):
    half = 0.5 * factor
    axis = kc.ndim - 2
    depth = kc.shape[axis]
    z = iota(kc.shape, axis)
    low, top = z == 0, z == depth - 1
    up = half * (kc + jnp.where(top, 0.0, turn(kc, -1, axis)))
    down = half * (kc + jnp.where(low, 0.0, turn(kc, 1, axis)))
    ahead = half * (kc + turn(kc, -1, axis + 1))
    behind = half * (kc + turn(kc, 1, axis + 1))
    right = half * (kc + kp)
    left = half * (kc + km)
    diagonal = up + down + ahead + behind + right + left
    inverse = jnp.where(kc > 0, 1.0 / diagonal, 0.0)
    up = jnp.where(top, 0.0, up)
    down = jnp.where(low, 0.0, down)
    weights = [w * inverse for w in (left, right, behind, ahead, down, up)]
    return weights, inverse, diagonal


def neighbour_sum(weights, below, centre, above):
    axis = centre.ndim - 2
    left, right, behind, ahead, down, up = weights
    total = left * below + right * above
    total = total + behind * turn(centre, 1, axis + 1) + ahead * turn(centre, -1, axis + 1)
    return total + down * turn(centre, 1, axis) + up * turn(centre, -1, axis)


def rows(low, high, body, chunk, unroll):
    full = (high - low) // chunk

    def step(n, carry):
        body(pl.ds(low + n * chunk, chunk), pl.ds(low + n * chunk - 1, chunk), pl.ds(low + n * chunk + 1, chunk))
        return carry

    lax.fori_loop(0, full, step, 0, unroll=unroll)
    at = low + full * chunk
    if at < high:
        body(pl.ds(at, high - at), pl.ds(at - 1, high - at), pl.ds(at + 1, high - at))


class Level:
    def __init__(self, k, weights, bh, x, p, factor, chunk, unroll):
        self.k, self.weights, self.bh, self.x, self.p, self.factor = k, weights, bh, x, p, factor
        self.chunk, self.unroll = chunk, unroll

    def rows(self, low, high, body):
        rows(low, high, body, self.chunk, self.unroll)

    def set_up(self, low, high, b, diagonal):
        def body(q, below, above):
            weights, inverse, diag = weights_row(self.k[q], self.k[below], self.k[above], self.factor)
            for n in range(6):
                self.weights[n, q] = weights[n]
            self.bh[q] = b[q] * inverse
            diagonal[q] = diag

        self.rows(low, high, body)

    def total(self, x, q, below, above):
        return neighbour_sum([self.weights[n, q] for n in range(6)], x[below], x[q], x[above])

    def pre(self, low, high):
        middle, ((c1, c2),) = chebyshev(2, LOW_BOUND)

        def body(q, below, above):
            first = self.bh[q]
            total = self.total(self.bh, q, below, above)
            self.x[q] = (1 / middle) * (1 + c1 - c2 + c2 * middle) * first + (c2 / middle) * total

        self.rows(low, high, body)

    def residue(self, low, high, diagonal, out, at):
        def body(q, below, above):
            value = diagonal[q] * (self.bh[q] - self.x[q] + self.total(self.x, q, below, above))
            out[pl.ds(q.start + (at - low), q.size)] = value

        self.rows(low, high, body)

    def post(self, low, high, out):
        middle, ((c1, c2),) = chebyshev(2, LOW_BOUND)

        def first(q, below, above):
            update = (self.bh[q] - self.x[q] + self.total(self.x, q, below, above)) * (1 / middle)
            self.p[q] = update
            out[q] = self.x[q] + update

        def second(q, below, above):
            residue = self.bh[q] - out[q] + self.total(out, q, below, above)
            self.x[q] = out[q] + c1 * self.p[q] + c2 * residue

        self.rows(low - 1, high + 1, first)
        self.rows(low, high, second)


def spec(n):
    return [pl.BlockSpec(memory_space=pltpu.VMEM)] * n


def call(body, outs, scratch, *args, hbm_in=0, hbm_out=0, sems=(), cost=None):
    args = [pltpu.with_memory_space_constraint(x, pltpu.HBM) if n < hbm_in else x for n, x in enumerate(args)]
    return pl.pallas_call(
        body,
        out_shape=[pltpu.HBM(s, F32) if n < hbm_out else jax.ShapeDtypeStruct(s, F32) for n, s in enumerate(outs)],
        in_specs=[pl.BlockSpec(memory_space=pltpu.HBM)] * hbm_in + spec(len(args) - hbm_in),
        out_specs=[pl.BlockSpec(memory_space=pltpu.HBM)] * hbm_out + spec(len(outs) - hbm_out),
        scratch_shapes=[pltpu.VMEM(s, F32) for s in scratch] + [pltpu.SemaphoreType.DMA(s) for s in sems],
        compiler_params=pltpu.CompilerParams(vmem_limit_bytes=VMEM_LIMIT),
        cost_estimate=cost,
    )(*args)


class Copies:
    def __init__(self, sems):
        self.sems, self.used = sems, 0

    def start(self, source, target):
        copy = pltpu.make_async_copy(source, target, self.sems.at[self.used])
        copy.start()
        self.used += 1
        return copy


def odd(axis):
    return lax.rem(lax.axis_index(axis), 2) == 1


def pieces(n, source, target, copies):
    size = source.shape[0] // n
    return [copies.start(source.at[pl.ds(i * size, size)], target.at[pl.ds(i * size, size)]) for i in range(n)]


def strip_kernel(b_any, k_any, own, xa, xb, b_ref, k_ref, sems):
    odd_x = odd("gx")
    arrays = ((k_ref, KX), (b_ref, BX))
    copies = Copies(sems)
    waits = [pieces(PIECES, k_any, k_ref, copies), pieces(PIECES, b_any, b_ref, copies)]
    at = 0
    for n, (ref, width) in enumerate(arrays):
        for copy in waits[n]:
            copy.wait()
        planes = [ref[pl.ds(i, 64, stride=8), :] for i in range(8)]
        for i in range(8):
            own[n, i] = planes[i]
        for i in range(width):
            first, last = planes[i], planes[8 - width + i]
            xa[at] = jnp.where(odd_x, first, last)
            xb[at] = jnp.where(odd_x, last, first)
            at += 1


def pack_kernel(own, xa, xb, k_out, b_out, ya, yb):
    odd_x, odd_y = odd("gx"), odd("gy")
    lane = iota((64, 128), 1)
    for n in range(KX + BX):
        a, b = xa[n], xb[n]
        left, right = jnp.where(odd_x, a, b), jnp.where(odd_x, b, a)
        if n < KX:
            k_out[n], k_out[8 + KX + n] = left, right
        else:
            b_out[n - KX], b_out[8 + BX + n - KX] = left, right
    for i in range(8):
        k_out[KX + i] = own[0, i]
        b_out[BX + i] = own[1, i]
    for n, (array, start, count, room) in enumerate(PACKED):
        ref, width = ((k_out, KY), (b_out, BY))[array]
        first, last = jnp.zeros((64, 128), F32), jnp.zeros((64, 128), F32)
        for i in range(count):
            plane = ref[start + i]
            here = (lane >= room * i) & (lane < room * i + width)
            first = jnp.where(here, turn(plane, room * i, 1), first)
            last = jnp.where(here, turn(plane, room * i + width, 1), last)
        ya[n] = jnp.where(odd_y, first, last)
        yb[n] = jnp.where(odd_y, last, first)


def first_kernel(
    count, k_rows, b_rows, ya, yb, k_hbm, b_hbm, x_hbm, k1_hbm, b1_hbm, x1_hbm, sa_hbm, sb_hbm, g_hbm,
    weights, bh, diagonal, x_out, k1, b1, x1, sa, sb, k_out, b_out, fine, wide, thin, w1, bh1, diagonal1, fine1, thin1, g_out, sems,
):
    copies = Copies(sems)
    flying = []
    odd_x, odd_y = odd("gx"), odd("gy")
    lane = iota((64, 128), 1)
    for n, (array, start, some, room) in enumerate(PACKED):
        a, b = ya[n], yb[n]
        left, right = jnp.where(odd_y, a, b), jnp.where(odd_y, b, a)
        rows_in, out, width, shift = ((k_rows, k_out, KY, 0), (b_rows, b_out, BY, 1))[array]
        for i in range(some):
            ahead, behind = turn(right, -room * i, 1), turn(left, 128 - width - room * i, 1)
            out[shift + start + i, :, 0:128] = rows_in[start + i]
            out[shift + start + i, :, 128:256] = jnp.where(lane < width, ahead, jnp.where(lane >= 128 - width, behind, 0.0))

    flying.append(copies.start(k_out.at[pl.ds(4, 14)], k_hbm))
    flying.append(copies.start(b_out.at[pl.ds(5, 12)], b_hbm))
    level = Level(k_out, weights, bh, x_out, None, 1.0, *SHAPE0)
    level.set_up(1, 21, b_out, diagonal)
    level.pre(2, 20)
    flying.append(copies.start(x_out.at[pl.ds(4, 14)], x_hbm))
    level.residue(3, 19, diagonal, fine, 0)
    for m in range(8):
        wide[m] = fine[2 * m] + fine[2 * m + 1]
    for m in range(10):
        wide[8 + m] = k_out[2 * m + 1] + k_out[2 * m + 2]
    thin[...] = dot(wide[...].reshape(18 * 64, 256), coarsen_matrix(256, 128, 140, 12, 0.125))
    for m in range(18):
        plane = thin[pl.ds(64 * m, 32, stride=2), :] + thin[pl.ds(64 * m + 1, 32, stride=2), :]
        if m < 8:
            b1[1 + m] = plane
        else:
            k1[m - 8] = plane

    level = Level(k1, w1, bh1, x1, None, 0.25, *SHAPE1)
    flying.append(copies.start(k1, k1_hbm))
    flying.append(copies.start(b1, b1_hbm))
    level.set_up(1, 9, b1, diagonal1)
    level.pre(2, 8)
    flying.append(copies.start(x1, x1_hbm))
    for n, (ref, to_right, to_left) in enumerate(((x1, 3, 4), (x1, 4, 5), (x1, 5, 6), (b1, 4, 5), (k1, 3, 6))):
        sa[n] = jnp.where(odd_x, ref[to_left], ref[to_right])
        sb[n] = jnp.where(odd_x, ref[to_right], ref[to_left])
    flying.append(copies.start(sa, sa_hbm))
    flying.append(copies.start(sb, sb_hbm))
    level.residue(3, 7, diagonal1, fine1, 0)
    parts = [fine1[0] + fine1[1], fine1[2] + fine1[3], k1[3] + k1[4], k1[5] + k1[6]]
    thin1[...] = dot(jnp.concatenate(parts, axis=0), coarsen_matrix(128, 128, 64, 0, 0.125))
    payload = jnp.zeros((16, 128), F32)
    for n in range(4):
        part = thin1[pl.ds(32 * n, 16, stride=2), :] + thin1[pl.ds(32 * n + 1, 16, stride=2), :]
        payload = payload + turn(part, 32 * n, 1)
    for n in range(count):
        g_out[n] = payload
    flying += pieces(PIECES, g_out, g_hbm, copies)
    for copy in flying:
        copy.wait()


def prepare_kernel(
    ra_hbm, rb_hbm, k1_hbm, b1_hbm, x1_hbm, k_hbm, b_hbm, x_hbm, w0, bh0, d0, x0, w1, bh1, x1,
    ra, rb, k1_in, b1_in, x1_in, k0, b0, k1, b1, d1, sems,
):
    odd_x = odd("gx")
    copies = Copies(sems)
    for_level0 = [copies.start(k_hbm, k0), copies.start(b_hbm, b0.at[pl.ds(1, 12)]), copies.start(x_hbm, x0)]
    for_level1 = [copies.start(*pair) for pair in ((ra_hbm, ra), (rb_hbm, rb), (k1_hbm, k1_in), (b1_hbm, b1_in), (x1_hbm, x1_in))]
    for copy in for_level1:
        copy.wait()
    for side in range(2):

        def pick(n):
            a, b = ra[n], rb[n]
            return jnp.where(odd_x, a, b) if side == 0 else jnp.where(odd_x, b, a)

        for n in range(3):
            x1[n if side == 0 else 9 + n] = pick(n)
        b1[1 if side == 0 else 10] = pick(3)
        k1[0 if side == 0 else 11] = pick(4)
    for n in range(6):
        x1[3 + n] = x1_in[2 + n]
    for n in range(8):
        b1[2 + n] = b1_in[1 + n]
    for n in range(10):
        k1[1 + n] = k1_in[n]
    Level(k1, w1, bh1, None, None, 0.25, *SHAPE1).set_up(1, 11, b1, d1)
    for copy in for_level0:
        copy.wait()
    Level(k0, w0, bh0, None, None, 1.0, *SHAPE0).set_up(1, 13, b0, d0)


def last_kernel(
    count, w0, bh0, d0, x0, w1, bh1, x1, g, ga, gb, pressure, residual,
    k2, b2, w2, bh2, x2, y2, p2, fine2, sums2, coarse2, t1, y1, p1, stack1, t0, y0, p0, stack0, pressure_rows, residual_rows, sems,
):
    copies = Copies(sems)
    odd_y = odd("gy")
    me = lax.axis_index("gx")
    lane = iota((16, 128), 1)

    def window(j, carry):
        device = me - 11 + j
        inside = (device >= 0) & (device < count)
        at = jnp.clip(device, 0, count - 1)
        own, a, b = g[at], ga[at], gb[at]
        left, right = jnp.where(odd_y, a, b), jnp.where(odd_y, b, a)
        for n, out in ((0, b2), (2, k2)):
            for m in range(2):
                s = -32 * (n + m)
                value = jnp.where(lane < 32, turn(own, s, 1), jnp.where(lane < 64, turn(right, s + 32, 1), jnp.where(lane >= 96, turn(left, s + 96, 1), 0.0)))
                out[2 * j + m] = jnp.where(inside, value, 0.0)
        return carry

    lax.fori_loop(0, 23, window, 0, unroll=WINDOW_UNROLL)
    level = Level(k2, w2, bh2, x2, p2, 0.0625, *SHAPE2)
    level.set_up(1, 45, b2, y2)
    level.pre(2, 44)
    level.residue(4, 42, y2, fine2, 4)
    zero = jnp.zeros((16, 128), F32)
    for m in (0, 1, 21, 22):
        sums2[m] = zero
    for m in range(2, 21):
        sums2[m] = fine2[2 * m] + fine2[2 * m + 1]
    for m in range(23):
        sums2[23 + m] = k2[2 * m] + k2[2 * m + 1]
    coarse2[...] = dot(sums2[...].reshape(46 * 16, 128), coarsen_matrix(128, 128, 64, 32, 0.125))
    both = coarse2[pl.ds(0, 46 * 8, stride=2), :] + coarse2[pl.ds(1, 46 * 8, stride=2), :]
    both = both.reshape(46, 8, 128)
    b3, k3 = both[:23], both[23:]
    none = jnp.zeros((1, 8, 128), F32)

    def after(value):
        return jnp.concatenate([value[1:], none], axis=0)

    def before(value):
        return jnp.concatenate([none, value[:-1]], axis=0)

    w3, inverse, _ = weights_row(k3, before(k3), after(k3), 0.015625)
    middle, steps = chebyshev(COARSE, COARSE_LOW)
    source = b3 * inverse
    update = source * (1 / middle)
    e3 = update
    for c1, c2 in steps:
        update = c1 * update + c2 * (source - e3 + neighbour_sum(w3, before(e3), e3, after(e3)))
        e3 = e3 + update

    tall = coarse2
    for m in range(5):
        for half in range(2):
            tall[pl.ds(16 * m + half, 8, stride=2), :] = e3[9 + m]
    fine = dot(tall[0 : 5 * 16, :], refine_matrix(128, 128, 64, 32))
    for m in range(10):
        part = fine[16 * (m // 2) : 16 * (m // 2) + 16]
        x2[18 + m] = x2[18 + m] + part
    level.post(20, 26, y2)

    for m in range(6):
        for half in range(2):
            stack1[pl.ds(32 * m + half, 16, stride=2), :] = x2[20 + m]
    fine = dot(stack1[...], refine_matrix(128, 128, 70, 6))
    for m in range(12):
        t1[m] = x1[m] + fine[32 * (m // 2) : 32 * (m // 2) + 32]
    level = Level(None, w1, bh1, t1, p1, 0.25, *SHAPE1)
    level.post(2, 10, y1)

    for m in range(8):
        for half in range(2):
            stack0[pl.ds(64 * m + half, 32, stride=2), :] = t1[2 + m]
    matrix = refine_matrix(128, 256, 140, 12)
    fine = dot(stack0[...], matrix)
    for m in range(14):
        row = (m + 1) // 2
        t0[m] = x0[m] + fine[64 * row : 64 * row + 64]
    level = Level(None, w0, bh0, t0, p0, 1.0, *SHAPE0)
    level.post(2, 12, y0)
    for i in range(8):
        pressure_rows[pl.ds(i, 64, stride=8), :] = t0[3 + i, :, 0:128]
    waits = pieces(PIECES, pressure_rows, pressure, copies)
    for i in range(8):
        q = 3 + i
        value = bh0[q] - t0[q] + level.total(t0, q, q - 1, q + 1)
        residual_rows[pl.ds(i, 64, stride=8), :] = (d0[q] * value)[:, 0:128]
    waits += pieces(PIECES, residual_rows, residual, copies)
    for copy in waits:
        copy.wait()


def on_device(right_side, conductivity):
    count = lax.axis_size("gx")
    b, k = right_side.reshape(512, 128), conductivity.reshape(512, 128)
    own, xa, xb = call(
        strip_kernel, [(2, 8, 64, 128)] + [(KX + BX, 64, 128)] * 2, [(512, 128)] * 2, b, k, hbm_in=2, sems=[(2 * PIECES,)]
    )
    xa, xb = swap(xa, "gx", 0), swap(xb, "gx", 1)
    k_rows, b_rows, ya, yb = call(
        pack_kernel, [(8 + 2 * KX, 64, 128), (8 + 2 * BX, 64, 128)] + [(len(PACKED), 64, 128)] * 2, [], own, xa, xb
    )
    ya, yb = swap(ya, "gy", 0), swap(yb, "gy", 1)
    rows0, rows1, rows2, rows3 = (22, 64, 256), (10, 32, 128), (46, 16, 128), (12, 32, 128)
    wide0 = (14, 64, 256)
    k0, b0, x0, k1, b1, x1, sa, sb, g = call(
        functools.partial(first_kernel, count),
        [wide0, (12, 64, 256), wide0, rows1, rows1, rows1, (5, 32, 128), (5, 32, 128), (count, 16, 128)],
        [(6,) + rows0, rows0, rows0, rows0, rows1, rows1, rows1, (5, 32, 128), (5, 32, 128)]
        + [rows0, rows0, (16, 64, 256), (18, 64, 256), (18 * 64, 128)]
        + [(6,) + rows1, rows1, rows1, (4, 32, 128), (128, 128), (count, 16, 128)],
        k_rows, b_rows, ya, yb,
        hbm_out=9,
        sems=[(8 + PIECES,)],
    )
    ra, rb = swap(sa, "gx", 0), swap(sb, "gx", 1)
    g = lax.all_to_all(g, "gx", 0, 0, tiled=True)
    g, ra, rb, k0, b0, x0, k1, b1, x1 = lax.optimization_barrier((g, ra, rb, k0, b0, x0, k1, b1, x1))
    ga, gb = swap(g, "gy", 0), swap(g, "gy", 1)
    kept = call(
        prepare_kernel,
        [(6,) + wide0, wide0, wide0, wide0, (6,) + rows3, rows3, rows3],
        [(5, 32, 128), (5, 32, 128), rows1, rows1, rows1, wide0, wide0, rows3, rows3, rows3],
        ra, rb, k1, b1, x1, k0, b0, x0,
        hbm_in=8,
        sems=[(8,)],
        cost=pl.CostEstimate(flops=20_000_000, bytes_accessed=8_000_000, transcendentals=200_000),
    )
    pressure, residual = call(
        functools.partial(last_kernel, count),
        [(512, 128)] * 2,
        [rows2, rows2, (6,) + rows2, rows2, rows2, rows2, rows2, rows2, rows2, (46 * 16, 128)]
        + [rows3, rows3, rows3, (6 * 32, 128)]
        + [wide0, wide0, wide0, (8 * 64, 128), (512, 128), (512, 128)],
        *kept, g, ga, gb,
        hbm_out=2,
        sems=[(2 * PIECES,)],
    )
    return pressure.reshape(64, 8, 128), residual.reshape(64, 8, 128)


def solution(mesh):
    place = P(None, "gx", "gy")
    return jax.shard_map(
        on_device, mesh=mesh, in_specs=(place, place), out_specs=(place, place), check_vma=False
    )
```

```python
import functools

import jax
import jax.numpy as jnp
from jax import lax
from jax.experimental import pallas as pl
from jax.experimental.pallas import tpu as pltpu
from jax.sharding import PartitionSpec as P

F32 = jnp.float32
COARSE = 8
LOW_BOUND = 0.3
HIGH_BOUND = 2.0
COARSE_LOW = 0.02
VMEM_LIMIT = 28 * 1024 * 1024

SHAPE0, SHAPE1, SHAPE2, WINDOW_UNROLL = (1,True), (4, True), (8, True), True

PIECES = 4

KX, BX, KY, BY = 7, 6, 13, 12
PACKED_K = ((0, 9, 14), (9, 9, 14), (18, 4, 14))
PACKED_B = ((0, 10, 12), (10, 10, 12))


def pairs(size, offset):
    found = []
    for i in range(offset, size - 1, 2):
        found += [(i, i + 1), (i + 1, i)]
    return found


def swap(value, axis, offset):
    return lax.ppermute(value, axis, pairs(lax.axis_size(axis), offset))


def chebyshev(sweeps, lower):
    middle = (HIGH_BOUND + lower) / 2
    half_width = (HIGH_BOUND - lower) / 2
    ratio = middle / half_width
    rho = 1 / ratio
    steps = []
    for _ in range(sweeps - 1):
        rho_next = 1 / (2 * ratio - rho)
        steps.append((rho_next * rho, 2 * rho_next / half_width))
        rho = rho_next
    return middle, steps


def iota(shape, axis):
    return lax.broadcasted_iota(jnp.int32, shape, axis)


def dot(a, b):
    b = b.astype(jnp.bfloat16)
    total = None
    for _ in range(3):
        piece = a.astype(jnp.bfloat16)
        a = a - piece.astype(F32)
        part = jnp.dot(piece, b, preferred_element_type=F32)
        total = part if total is None else total + part
    return total


def coarsen_matrix(fine, coarse, right, left, scale):
    f, c = iota((fine, coarse), 0), iota((fine, coarse), 1)
    ahead = (f < right) & (c == lax.shift_right_logical(f, 1))
    behind = (f >= fine - left) & (coarse - c == lax.shift_right_logical(fine - f + 1, 1))
    return jnp.where(ahead | behind, scale, 0.0).astype(F32)


def refine_matrix(coarse, fine, right, left):
    c, f = iota((coarse, fine), 0), iota((coarse, fine), 1)
    ahead = (f < right) & (c == lax.shift_right_logical(f, 1))
    behind = (f >= fine - left) & (coarse - c == lax.shift_right_logical(fine - f + 1, 1))
    return jnp.where(ahead | behind, 1.0, 0.0).astype(F32)


def turn(value, shift, axis):
    shift = shift % value.shape[axis]
    return value if shift == 0 else pltpu.roll(value, shift, axis=axis)


def edged(value, axis, top):
    depth = value.shape[axis]
    cut = functools.partial(lax.slice_in_dim, value, axis=axis)
    index = iota(value.shape[:axis] + (8,) + value.shape[axis + 1 :], axis)
    if top:
        edge = jnp.where(index == 7, 0.0, cut(depth - 8, depth))
        return edge if depth == 8 else jnp.concatenate([cut(0, depth - 8), edge], axis=axis)
    edge = jnp.where(index == 0, 0.0, cut(0, 8))
    return edge if depth == 8 else jnp.concatenate([edge, cut(8, depth)], axis=axis)


def weights_row(kc, km, kp, factor):
    axis = kc.ndim - 2
    up = kc + edged(turn(kc, -1, axis), axis, True)
    down = kc + edged(turn(kc, 1, axis), axis, False)
    ahead = kc + turn(kc, -1, axis + 1)
    behind = kc + turn(kc, 1, axis + 1)
    right = kc + kp
    left = kc + km
    diagonal = (up + down) + (ahead + behind) + (right + left)
    inverse = jnp.where(kc > 0, 1.0 / diagonal, 0.0)
    weights = [w * inverse for w in (left, right, behind, ahead, edged(down, axis, False), edged(up, axis, True))]
    return weights, inverse * (2.0 / factor), diagonal * (0.5 * factor)


def neighbour_sum(weights, below, centre, above):
    axis = centre.ndim - 2
    left, right, behind, ahead, down, up = weights
    total = left * below + right * above
    total = total + behind * turn(centre, 1, axis + 1) + ahead * turn(centre, -1, axis + 1)
    return total + down * turn(centre, 1, axis) + up * turn(centre, -1, axis)


def rows(low, high, body, chunk, unroll):
    full = (high - low) // chunk

    def step(n, carry):
        body(pl.ds(low + n * chunk, chunk), pl.ds(low + n * chunk - 1, chunk), pl.ds(low + n * chunk + 1, chunk))
        return carry

    lax.fori_loop(0, full, step, 0, unroll=unroll)
    at = low + full * chunk
    if at < high:
        body(pl.ds(at, high - at), pl.ds(at - 1, high - at), pl.ds(at + 1, high - at))


class Level:
    def __init__(self, k, weights, bh, x, p, factor, chunk, unroll):
        self.k, self.weights, self.bh, self.x, self.p, self.factor = k, weights, bh, x, p, factor
        self.chunk, self.unroll = chunk, unroll

    def rows(self, low, high, body):
        rows(low, high, body, self.chunk, self.unroll)

    def set_up(self, low, high, b=None, diagonal=None, inverses=None):
        def body(q, below, above):
            weights, inverse, diag = weights_row(self.k[q], self.k[below], self.k[above], self.factor)
            for n in range(6):
                self.weights[n, q] = weights[n]
            if b is not None:
                self.bh[q] = b[q] * inverse
            if inverses is not None:
                inverses[q] = inverse
            if diagonal is not None:
                diagonal[q] = diag

        self.rows(low, high, body)

    def total(self, x, q, below, above):
        return neighbour_sum([self.weights[n, q] for n in range(6)], x[below], x[q], x[above])

    def pre(self, low, high):
        middle, ((c1, c2),) = chebyshev(2, LOW_BOUND)

        def body(q, below, above):
            first = self.bh[q]
            total = self.total(self.bh, q, below, above)
            self.x[q] = (1 / middle) * (1 + c1 - c2 + c2 * middle) * first + (c2 / middle) * total

        self.rows(low, high, body)

    def residue(self, low, high, diagonal, out, at):
        def body(q, below, above):
            value = diagonal[q] * (self.bh[q] - self.x[q] + self.total(self.x, q, below, above))
            out[pl.ds(q.start + (at - low), q.size)] = value

        self.rows(low, high, body)

    def post(self, low, high, out):
        middle, ((c1, c2),) = chebyshev(2, LOW_BOUND)

        def first(q, below, above):
            update = (self.bh[q] - self.x[q] + self.total(self.x, q, below, above)) * (1 / middle)
            self.p[q] = update
            out[q] = self.x[q] + update

        def second(q, below, above):
            residue = self.bh[q] - out[q] + self.total(out, q, below, above)
            self.x[q] = out[q] + c1 * self.p[q] + c2 * residue

        self.rows(low - 1, high + 1, first)
        self.rows(low, high, second)


def spec(n):
    return [pl.BlockSpec(memory_space=pltpu.VMEM)] * n


def call(body, outs, scratch, *args, hbm_in=0, hbm_out=0, sems=(), cost=None):
    args = [pltpu.with_memory_space_constraint(x, pltpu.HBM) if n < hbm_in else x for n, x in enumerate(args)]
    return pl.pallas_call(
        body,
        out_shape=[pltpu.HBM(s, F32) if n < hbm_out else jax.ShapeDtypeStruct(s, F32) for n, s in enumerate(outs)],
        in_specs=[pl.BlockSpec(memory_space=pltpu.HBM)] * hbm_in + spec(len(args) - hbm_in),
        out_specs=[pl.BlockSpec(memory_space=pltpu.HBM)] * hbm_out + spec(len(outs) - hbm_out),
        scratch_shapes=[pltpu.VMEM(s, F32) for s in scratch] + [pltpu.SemaphoreType.DMA(s) for s in sems],
        compiler_params=pltpu.CompilerParams(vmem_limit_bytes=VMEM_LIMIT),
        cost_estimate=cost,
    )(*args)


class Copies:
    def __init__(self, sems):
        self.sems, self.used = sems, 0

    def start(self, source, target):
        copy = pltpu.make_async_copy(source, target, self.sems.at[self.used])
        copy.start()
        self.used += 1
        return copy


def odd(axis):
    return lax.rem(lax.axis_index(axis), 2) == 1


def pieces(n, source, target, copies):
    size = source.shape[0] // n
    return [copies.start(source.at[pl.ds(i * size, size)], target.at[pl.ds(i * size, size)]) for i in range(n)]


def strip_kernel(k_any, b_any, own_k, own_b, xka, xkb, xba, xbb, k_ref, b_ref, sems):
    odd_x = odd("gx")
    copies = Copies(sems)
    waits = [pieces(PIECES, k_any, k_ref, copies), pieces(PIECES, b_any, b_ref, copies)]
    for n, (ref, own, xa, xb, width) in enumerate(((k_ref, own_k, xka, xkb, KX), (b_ref, own_b, xba, xbb, BX))):
        for copy in waits[n]:
            copy.wait()
        planes = [ref[pl.ds(i, 64, stride=8), :] for i in range(8)]
        for i in range(8):
            own[i] = planes[i]
        for i in range(width):
            first, last = planes[i], planes[8 - width + i]
            xa[i] = jnp.where(odd_x, first, last)
            xb[i] = jnp.where(odd_x, last, first)


def pack_kernel(packed, width, own, xa, xb, rows_out, ya, yb):
    odd_x, odd_y = odd("gx"), odd("gy")
    lane = iota((64, 128), 1)
    halo = xa.shape[0]
    planes = [None] * (8 + 2 * halo)
    for n in range(halo):
        a, b = xa[n], xb[n]
        planes[n], planes[8 + halo + n] = jnp.where(odd_x, a, b), jnp.where(odd_x, b, a)
    for i in range(8):
        planes[halo + i] = own[i]
    for n, plane in enumerate(planes):
        rows_out[n] = plane
    for n, (start, count, room) in enumerate(packed):
        first, last = jnp.zeros((64, 128), F32), jnp.zeros((64, 128), F32)
        for i in range(count):
            plane = planes[start + i]
            here = (lane >= room * i) & (lane < room * i + width)
            first = jnp.where(here, turn(plane, room * i, 1), first)
            last = jnp.where(here, turn(plane, room * i + width, 1), last)
        ya[n] = jnp.where(odd_y, first, last)
        yb[n] = jnp.where(odd_y, last, first)


def outer_columns(packed, width, ya, yb):
    odd_y = odd("gy")
    lane = iota((64, 128), 1)
    for n, (start, count, room) in enumerate(packed):
        a, b = ya[n], yb[n]
        left, right = jnp.where(odd_y, a, b), jnp.where(odd_y, b, a)
        for i in range(count):
            ahead, behind = turn(right, -room * i, 1), turn(left, 128 - width - room * i, 1)
            yield start + i, jnp.where(lane < width, ahead, jnp.where(lane >= 128 - width, behind, 0.0))


def weights_kernel(
    k_rows, ya, yb, k_hbm, k1_hbm, weights, inverse, diagonal, k1, w1, inverse1, diagonal1, k_out, wide, thin, sems,
):
    copies = Copies(sems)
    for q, outer in outer_columns(PACKED_K, KY, ya, yb):
        k_out[q, :, 0:128] = k_rows[q]
        k_out[q, :, 128:256] = outer
    flying = [copies.start(k_out.at[pl.ds(4, 14)], k_hbm)]
    for m in range(10):
        wide[m] = k_out[2 * m + 1] + k_out[2 * m + 2]
    thin[...] = dot(wide[...].reshape(10 * 64, 256), coarsen_matrix(256, 128, 140, 12, 0.125))
    for m in range(10):
        k1[m] = thin[pl.ds(64 * m, 32, stride=2), :] + thin[pl.ds(64 * m + 1, 32, stride=2), :]
    flying.append(copies.start(k1, k1_hbm))
    Level(k_out, weights, None, None, None, 1.0, *SHAPE0).set_up(1, 21, None, diagonal, inverse)
    Level(k1, w1, None, None, None, 0.25, *SHAPE1).set_up(1, 9, None, diagonal1, inverse1)
    for copy in flying:
        copy.wait()


def first_kernel(
    count, b_rows, ya, yb, weights, inverse, diagonal, k1, w1, inverse1, diagonal1,
    bh_hbm, x_hbm, b1_hbm, x1_hbm, sa_hbm, sb_hbm, g_hbm,
    bh, x_out, b1, bh1, x1, sa, sb, fine, wide, thin, fine1, thin1, g_out, sems,
):
    odd_x = odd("gx")
    copies = Copies(sems)
    for n, outer in outer_columns(PACKED_B, BY, ya, yb):
        q = n + 1
        bh[q, :, 0:128] = b_rows[n] * inverse[q, :, 0:128]
        bh[q, :, 128:256] = outer * inverse[q, :, 128:256]
    flying = [copies.start(bh.at[pl.ds(5, 12)], bh_hbm)]
    level = Level(None, weights, bh, x_out, None, 1.0, *SHAPE0)
    level.pre(2, 20)
    flying.append(copies.start(x_out.at[pl.ds(4, 14)], x_hbm))
    level.residue(3, 19, diagonal, fine, 0)
    for m in range(8):
        wide[m] = fine[2 * m] + fine[2 * m + 1]
    thin[...] = dot(wide[...].reshape(8 * 64, 256), coarsen_matrix(256, 128, 140, 12, 0.125))
    for m in range(8):
        b1[1 + m] = thin[pl.ds(64 * m, 32, stride=2), :] + thin[pl.ds(64 * m + 1, 32, stride=2), :]
        bh1[1 + m] = b1[1 + m] * inverse1[1 + m]
    flying.append(copies.start(b1, b1_hbm))

    level = Level(None, w1, bh1, x1, None, 0.25, *SHAPE1)
    level.pre(2, 8)
    flying.append(copies.start(x1, x1_hbm))
    for n, (ref, to_right, to_left) in enumerate(((x1, 3, 4), (x1, 4, 5), (x1, 5, 6), (b1, 4, 5), (k1, 3, 6))):
        sa[n] = jnp.where(odd_x, ref[to_left], ref[to_right])
        sb[n] = jnp.where(odd_x, ref[to_right], ref[to_left])
    flying.append(copies.start(sa, sa_hbm))
    flying.append(copies.start(sb, sb_hbm))
    level.residue(3, 7, diagonal1, fine1, 0)
    parts = [fine1[0] + fine1[1], fine1[2] + fine1[3], k1[3] + k1[4], k1[5] + k1[6]]
    thin1[...] = dot(jnp.concatenate(parts, axis=0), coarsen_matrix(128, 128, 64, 0, 0.125))
    payload = jnp.zeros((16, 128), F32)
    for n in range(4):
        part = thin1[pl.ds(32 * n, 16, stride=2), :] + thin1[pl.ds(32 * n + 1, 16, stride=2), :]
        payload = payload + turn(part, 32 * n, 1)
    for n in range(count):
        g_out[n] = payload
    flying += pieces(PIECES, g_out, g_hbm, copies)
    for copy in flying:
        copy.wait()


def prepare_kernel(
    ra_hbm, rb_hbm, k1_hbm, b1_hbm, x1_hbm, k_hbm, bh_hbm, x_hbm, w0, bh0, d0, x0, w1, bh1, x1,
    ra, rb, k1_in, b1_in, x1_in, k0, k1, b1, sems,
):
    odd_x = odd("gx")
    copies = Copies(sems)
    for_level0 = [copies.start(k_hbm, k0), copies.start(bh_hbm, bh0.at[pl.ds(1, 12)]), copies.start(x_hbm, x0)]
    for_level1 = [copies.start(*pair) for pair in ((ra_hbm, ra), (rb_hbm, rb), (k1_hbm, k1_in), (b1_hbm, b1_in), (x1_hbm, x1_in))]
    for copy in for_level1:
        copy.wait()
    for side in range(2):

        def pick(n):
            a, b = ra[n], rb[n]
            return jnp.where(odd_x, a, b) if side == 0 else jnp.where(odd_x, b, a)

        for n in range(3):
            x1[n if side == 0 else 9 + n] = pick(n)
        b1[1 if side == 0 else 10] = pick(3)
        k1[0 if side == 0 else 11] = pick(4)
    for n in range(6):
        x1[3 + n] = x1_in[2 + n]
    for n in range(8):
        b1[2 + n] = b1_in[1 + n]
    for n in range(10):
        k1[1 + n] = k1_in[n]
    Level(k1, w1, bh1, None, None, 0.25, *SHAPE1).set_up(1, 11, b1)
    for copy in for_level0:
        copy.wait()
    Level(k0, w0, None, None, None, 1.0, *SHAPE0).set_up(1, 13, None, d0)


def last_kernel(
    count, w0, bh0, d0, x0, w1, bh1, x1, g, ga, gb, pressure, residual,
    k2, b2, w2, bh2, x2, y2, p2, fine2, sums2, coarse2, t1, y1, p1, stack1, t0, y0, p0, stack0, pressure_rows, residual_rows, sems,
):
    copies = Copies(sems)
    odd_y = odd("gy")
    me = lax.axis_index("gx")
    lane = iota((16, 128), 1)

    def window(j, carry):
        device = me - 11 + j
        inside = (device >= 0) & (device < count)
        at = jnp.clip(device, 0, count - 1)
        own, a, b = g[at], ga[at], gb[at]
        left, right = jnp.where(odd_y, a, b), jnp.where(odd_y, b, a)
        for n, out in ((0, b2), (2, k2)):
            for m in range(2):
                s = -32 * (n + m)
                value = jnp.where(lane < 32, turn(own, s, 1), jnp.where(lane < 64, turn(right, s + 32, 1), jnp.where(lane >= 96, turn(left, s + 96, 1), 0.0)))
                out[2 * j + m] = jnp.where(inside, value, 0.0)
        return carry

    lax.fori_loop(0, 23, window, 0, unroll=WINDOW_UNROLL)
    level = Level(k2, w2, bh2, x2, p2, 0.0625, *SHAPE2)
    level.set_up(1, 45, b2, y2)
    level.pre(2, 44)
    level.residue(4, 42, y2, fine2, 4)
    zero = jnp.zeros((16, 128), F32)
    for m in (0, 1, 21, 22):
        sums2[m] = zero
    for m in range(2, 21):
        sums2[m] = fine2[2 * m] + fine2[2 * m + 1]
    for m in range(23):
        sums2[23 + m] = k2[2 * m] + k2[2 * m + 1]
    coarse2[...] = dot(sums2[...].reshape(46 * 16, 128), coarsen_matrix(128, 128, 64, 32, 0.125))
    both = coarse2[pl.ds(0, 46 * 8, stride=2), :] + coarse2[pl.ds(1, 46 * 8, stride=2), :]
    both = both.reshape(46, 8, 128)
    b3, k3 = both[:23], both[23:]
    none = jnp.zeros((1, 8, 128), F32)

    def after(value):
        return jnp.concatenate([value[1:], none], axis=0)

    def before(value):
        return jnp.concatenate([none, value[:-1]], axis=0)

    w3, inverse, _ = weights_row(k3, before(k3), after(k3), 0.015625)
    middle, steps = chebyshev(COARSE, COARSE_LOW)
    source = b3 * inverse
    update = source * (1 / middle)
    e3 = update
    for c1, c2 in steps:
        update = c1 * update + c2 * (source - e3 + neighbour_sum(w3, before(e3), e3, after(e3)))
        e3 = e3 + update

    tall = coarse2
    for m in range(5):
        for half in range(2):
            tall[pl.ds(16 * m + half, 8, stride=2), :] = e3[9 + m]
    fine = dot(tall[0 : 5 * 16, :], refine_matrix(128, 128, 64, 32))
    for m in range(10):
        part = fine[16 * (m // 2) : 16 * (m // 2) + 16]
        x2[18 + m] = x2[18 + m] + part
    level.post(20, 26, y2)

    for m in range(6):
        for half in range(2):
            stack1[pl.ds(32 * m + half, 16, stride=2), :] = x2[20 + m]
    fine = dot(stack1[...], refine_matrix(128, 128, 70, 6))
    for m in range(12):
        t1[m] = x1[m] + fine[32 * (m // 2) : 32 * (m // 2) + 32]
    level = Level(None, w1, bh1, t1, p1, 0.25, *SHAPE1)
    level.post(2, 10, y1)

    for m in range(8):
        for half in range(2):
            stack0[pl.ds(64 * m + half, 32, stride=2), :] = t1[2 + m]
    matrix = refine_matrix(128, 256, 140, 12)
    fine = dot(stack0[...], matrix)
    for m in range(14):
        row = (m + 1) // 2
        t0[m] = x0[m] + fine[64 * row : 64 * row + 64]
    level = Level(None, w0, bh0, t0, p0, 1.0, *SHAPE0)
    level.post(2, 12, y0)
    for i in range(8):
        pressure_rows[pl.ds(i, 64, stride=8), :] = t0[3 + i, :, 0:128]
    waits = pieces(PIECES, pressure_rows, pressure, copies)
    for i in range(8):
        q = 3 + i
        value = bh0[q] - t0[q] + level.total(t0, q, q - 1, q + 1)
        residual_rows[pl.ds(i, 64, stride=8), :] = (d0[q] * value)[:, 0:128]
    waits += pieces(PIECES, residual_rows, residual, copies)
    for copy in waits:
        copy.wait()


def on_device(right_side, conductivity):
    count = lax.axis_size("gx")
    b, k = right_side.reshape(512, 128), conductivity.reshape(512, 128)
    plane = (64, 128)
    own_k, own_b, xka, xkb, xba, xbb = call(
        strip_kernel,
        [(8,) + plane] * 2 + [(KX,) + plane] * 2 + [(BX,) + plane] * 2,
        [(512, 128)] * 2,
        k, b,
        hbm_in=2,
        sems=[(2 * PIECES,)],
    )
    xka, xkb = swap(xka, "gx", 0), swap(xkb, "gx", 1)
    xba, xbb = swap(xba, "gx", 0), swap(xbb, "gx", 1)

    def packed(own, xa, xb, pack, width):
        rows_out, ya, yb = call(
            functools.partial(pack_kernel, pack, width),
            [(8 + 2 * xa.shape[0],) + plane] + [(len(pack),) + plane] * 2,
            [],
            own, xa, xb,
            cost=pl.CostEstimate(flops=1_000_000, bytes_accessed=2_000_000, transcendentals=0),
        )
        return rows_out, swap(ya, "gy", 0), swap(yb, "gy", 1)

    rows0, rows1, rows2, rows3 = (22, 64, 256), (10, 32, 128), (46, 16, 128), (12, 32, 128)
    wide0 = (14, 64, 256)
    k0, k1, *about_k = call(
        weights_kernel,
        [wide0, rows1, (6,) + rows0, rows0, rows0, rows1, (6,) + rows1, rows1, rows1],
        [rows0, (10, 64, 256), (10 * 64, 128)],
        *packed(own_k, xka, xkb, PACKED_K, KY),
        hbm_out=2,
        sems=[(2,)],
        cost=pl.CostEstimate(flops=20_000_000, bytes_accessed=8_000_000, transcendentals=300_000),
    )
    bh0, x0, b1, x1, sa, sb, g = call(
        functools.partial(first_kernel, count),
        [(12, 64, 256), wide0, rows1, rows1, (5, 32, 128), (5, 32, 128), (count, 16, 128)],
        [rows0, rows0, rows1, rows1, rows1, (5, 32, 128), (5, 32, 128)]
        + [(16, 64, 256), (8, 64, 256), (8 * 64, 128), (4, 32, 128), (128, 128), (count, 16, 128)],
        *packed(own_b, xba, xbb, PACKED_B, BY), *about_k,
        hbm_out=7,
        sems=[(6 + PIECES,)],
    )
    ra, rb = swap(sa, "gx", 0), swap(sb, "gx", 1)
    g = lax.all_to_all(g, "gx", 0, 0, tiled=True)
    g, ra, rb, k0, bh0, x0, k1, b1, x1 = lax.optimization_barrier((g, ra, rb, k0, bh0, x0, k1, b1, x1))
    ga, gb = swap(g, "gy", 0), swap(g, "gy", 1)
    kept = call(
        prepare_kernel,
        [(6,) + wide0, wide0, wide0, wide0, (6,) + rows3, rows3, rows3],
        [(5, 32, 128), (5, 32, 128), rows1, rows1, rows1, wide0, rows3, rows3],
        ra, rb, k1, b1, x1, k0, bh0, x0,
        hbm_in=8,
        sems=[(8,)],
        cost=pl.CostEstimate(flops=20_000_000, bytes_accessed=8_000_000, transcendentals=200_000),
    )
    pressure, residual = call(
        functools.partial(last_kernel, count),
        [(512, 128)] * 2,
        [rows2, rows2, (6,) + rows2, rows2, rows2, rows2, rows2, rows2, rows2, (46 * 16, 128)]
        + [rows3, rows3, rows3, (6 * 32, 128)]
        + [wide0, wide0, wide0, (8 * 64, 128), (512, 128), (512, 128)],
        *kept, g, ga, gb,
        hbm_out=2,
        sems=[(2 * PIECES,)],
    )
    return pressure.reshape(64, 8, 128), residual.reshape(64, 8, 128)


def solution(mesh):
    place = P(None, "gx", "gy")
    return jax.shard_map(
        on_device, mesh=mesh, in_specs=(place, place), out_specs=(place, place), check_vma=False
    )
```

```python
import functools

import jax
import jax.numpy as jnp
from jax import lax
from jax.experimental import pallas as pl
from jax.experimental.pallas import tpu as pltpu
from jax.sharding import PartitionSpec as P

F32 = jnp.float32
COARSE = 8
LOW_BOUND = 0.3
HIGH_BOUND = 2.0
COARSE_LOW = 0.02
VMEM_LIMIT = 28 * 1024 * 1024

SHAPE0, SHAPE1, SHAPE2, WINDOW_UNROLL = (1,True), (4, True), (8, True), True

WINDOW = 23

PIECES = 4

KX, BX, KY, BY = 7, 6, 13, 12
PACKED_K = ((0, 9, 14), (9, 9, 14), (18, 4, 14))
PACKED_B = ((0, 10, 12), (10, 10, 12))


def pairs(size, offset):
    found = []
    for i in range(offset, size - 1, 2):
        found += [(i, i + 1), (i + 1, i)]
    return found


def swap(value, axis, offset):
    return lax.ppermute(value, axis, pairs(lax.axis_size(axis), offset))


def chebyshev(sweeps, lower):
    middle = (HIGH_BOUND + lower) / 2
    half_width = (HIGH_BOUND - lower) / 2
    ratio = middle / half_width
    rho = 1 / ratio
    steps = []
    for _ in range(sweeps - 1):
        rho_next = 1 / (2 * ratio - rho)
        steps.append((rho_next * rho, 2 * rho_next / half_width))
        rho = rho_next
    return middle, steps


def iota(shape, axis):
    return lax.broadcasted_iota(jnp.int32, shape, axis)


def dot(a, b):
    b = b.astype(jnp.bfloat16)
    total = None
    for _ in range(3):
        piece = a.astype(jnp.bfloat16)
        a = a - piece.astype(F32)
        part = jnp.dot(piece, b, preferred_element_type=F32)
        total = part if total is None else total + part
    return total


def coarsen_matrix(fine, coarse, right, left, scale):
    f, c = iota((fine, coarse), 0), iota((fine, coarse), 1)
    ahead = (f < right) & (c == lax.shift_right_logical(f, 1))
    behind = (f >= fine - left) & (coarse - c == lax.shift_right_logical(fine - f + 1, 1))
    return jnp.where(ahead | behind, scale, 0.0).astype(F32)


def refine_matrix(coarse, fine, right, left):
    c, f = iota((coarse, fine), 0), iota((coarse, fine), 1)
    ahead = (f < right) & (c == lax.shift_right_logical(f, 1))
    behind = (f >= fine - left) & (coarse - c == lax.shift_right_logical(fine - f + 1, 1))
    return jnp.where(ahead | behind, 1.0, 0.0).astype(F32)


def turn(value, shift, axis):
    shift = shift % value.shape[axis]
    return value if shift == 0 else pltpu.roll(value, shift, axis=axis)


def edged(value, axis, top):
    depth = value.shape[axis]
    cut = functools.partial(lax.slice_in_dim, value, axis=axis)
    index = iota(value.shape[:axis] + (8,) + value.shape[axis + 1 :], axis)
    if top:
        edge = jnp.where(index == 7, 0.0, cut(depth - 8, depth))
        return edge if depth == 8 else jnp.concatenate([cut(0, depth - 8), edge], axis=axis)
    edge = jnp.where(index == 0, 0.0, cut(0, 8))
    return edge if depth == 8 else jnp.concatenate([edge, cut(8, depth)], axis=axis)


def weights_row(kc, km, kp, factor):
    axis = kc.ndim - 2
    up = kc + edged(turn(kc, -1, axis), axis, True)
    down = kc + edged(turn(kc, 1, axis), axis, False)
    ahead = kc + turn(kc, -1, axis + 1)
    behind = kc + turn(kc, 1, axis + 1)
    right = kc + kp
    left = kc + km
    diagonal = (up + down) + (ahead + behind) + (right + left)
    inverse = jnp.where(kc > 0, 1.0 / diagonal, 0.0)
    weights = [w * inverse for w in (left, right, behind, ahead, edged(down, axis, False), edged(up, axis, True))]
    return weights, inverse * (2.0 / factor), diagonal * (0.5 * factor)


def neighbour_sum(weights, below, centre, above):
    axis = centre.ndim - 2
    left, right, behind, ahead, down, up = weights
    total = left * below + right * above
    total = total + behind * turn(centre, 1, axis + 1) + ahead * turn(centre, -1, axis + 1)
    return total + down * turn(centre, 1, axis) + up * turn(centre, -1, axis)


def rows(low, high, body, chunk, unroll):
    full = (high - low) // chunk

    def step(n, carry):
        body(pl.ds(low + n * chunk, chunk), pl.ds(low + n * chunk - 1, chunk), pl.ds(low + n * chunk + 1, chunk))
        return carry

    lax.fori_loop(0, full, step, 0, unroll=unroll)
    at = low + full * chunk
    if at < high:
        body(pl.ds(at, high - at), pl.ds(at - 1, high - at), pl.ds(at + 1, high - at))


class Level:
    def __init__(self, k, weights, bh, x, p, factor, chunk, unroll):
        self.k, self.weights, self.bh, self.x, self.p, self.factor = k, weights, bh, x, p, factor
        self.chunk, self.unroll = chunk, unroll

    def rows(self, low, high, body):
        rows(low, high, body, self.chunk, self.unroll)

    def set_up(self, low, high, b=None, diagonal=None, inverses=None):
        def body(q, below, above):
            weights, inverse, diag = weights_row(self.k[q], self.k[below], self.k[above], self.factor)
            for n in range(6):
                self.weights[n, q] = weights[n]
            if b is not None:
                self.bh[q] = b[q] * inverse
            if inverses is not None:
                inverses[q] = inverse
            if diagonal is not None:
                diagonal[q] = diag

        self.rows(low, high, body)

    def total(self, x, q, below, above):
        return neighbour_sum([self.weights[n, q] for n in range(6)], x[below], x[q], x[above])

    def pre(self, low, high):
        middle, ((c1, c2),) = chebyshev(2, LOW_BOUND)

        def body(q, below, above):
            first = self.bh[q]
            total = self.total(self.bh, q, below, above)
            self.x[q] = (1 / middle) * (1 + c1 - c2 + c2 * middle) * first + (c2 / middle) * total

        self.rows(low, high, body)

    def residue(self, low, high, diagonal, out, at):
        def body(q, below, above):
            value = diagonal[q] * (self.bh[q] - self.x[q] + self.total(self.x, q, below, above))
            out[pl.ds(q.start + (at - low), q.size)] = value

        self.rows(low, high, body)

    def post(self, low, high, out):
        middle, ((c1, c2),) = chebyshev(2, LOW_BOUND)

        def first(q, below, above):
            update = (self.bh[q] - self.x[q] + self.total(self.x, q, below, above)) * (1 / middle)
            self.p[q] = update
            out[q] = self.x[q] + update

        def second(q, below, above):
            residue = self.bh[q] - out[q] + self.total(out, q, below, above)
            self.x[q] = out[q] + c1 * self.p[q] + c2 * residue

        self.rows(low - 1, high + 1, first)
        self.rows(low, high, second)


def spec(n):
    return [pl.BlockSpec(memory_space=pltpu.VMEM)] * n


def call(body, outs, scratch, *args, hbm_in=0, hbm_out=0, sems=(), cost=None):
    args = [pltpu.with_memory_space_constraint(x, pltpu.HBM) if n < hbm_in else x for n, x in enumerate(args)]
    return pl.pallas_call(
        body,
        out_shape=[pltpu.HBM(s, F32) if n < hbm_out else jax.ShapeDtypeStruct(s, F32) for n, s in enumerate(outs)],
        in_specs=[pl.BlockSpec(memory_space=pltpu.HBM)] * hbm_in + spec(len(args) - hbm_in),
        out_specs=[pl.BlockSpec(memory_space=pltpu.HBM)] * hbm_out + spec(len(outs) - hbm_out),
        scratch_shapes=[pltpu.VMEM(s, F32) for s in scratch] + [pltpu.SemaphoreType.DMA(s) for s in sems],
        compiler_params=pltpu.CompilerParams(vmem_limit_bytes=VMEM_LIMIT),
        cost_estimate=cost,
    )(*args)


class Copies:
    def __init__(self, sems):
        self.sems, self.used = sems, 0

    def start(self, source, target):
        copy = pltpu.make_async_copy(source, target, self.sems.at[self.used])
        copy.start()
        self.used += 1
        return copy


def odd(axis):
    return lax.rem(lax.axis_index(axis), 2) == 1


def pieces(n, source, target, copies):
    size = source.shape[0] // n
    return [copies.start(source.at[pl.ds(i * size, size)], target.at[pl.ds(i * size, size)]) for i in range(n)]


def strip_kernel(width, source, own, xa, xb, ref, sems):
    odd_x = odd("gx")
    for copy in pieces(PIECES, source, ref, Copies(sems)):
        copy.wait()
    planes = [ref[pl.ds(i, 64, stride=8), :] for i in range(8)]
    for i in range(8):
        own[i] = planes[i]
    for i in range(width):
        first, last = planes[i], planes[8 - width + i]
        xa[i] = jnp.where(odd_x, first, last)
        xb[i] = jnp.where(odd_x, last, first)


def pack_kernel(packed, width, own, xa, xb, rows_out, ya, yb):
    odd_x, odd_y = odd("gx"), odd("gy")
    lane = iota((64, 128), 1)
    halo = xa.shape[0]
    planes = [None] * (8 + 2 * halo)
    for n in range(halo):
        a, b = xa[n], xb[n]
        planes[n], planes[8 + halo + n] = jnp.where(odd_x, a, b), jnp.where(odd_x, b, a)
    for i in range(8):
        planes[halo + i] = own[i]
    for n, plane in enumerate(planes):
        rows_out[n] = plane
    for n, (start, count, room) in enumerate(packed):
        first, last = jnp.zeros((64, 128), F32), jnp.zeros((64, 128), F32)
        for i in range(count):
            plane = planes[start + i]
            here = (lane >= room * i) & (lane < room * i + width)
            first = jnp.where(here, turn(plane, room * i, 1), first)
            last = jnp.where(here, turn(plane, room * i + width, 1), last)
        ya[n] = jnp.where(odd_y, first, last)
        yb[n] = jnp.where(odd_y, last, first)


def outer_columns(packed, width, ya, yb):
    odd_y = odd("gy")
    lane = iota((64, 128), 1)
    for n, (start, count, room) in enumerate(packed):
        a, b = ya[n], yb[n]
        left, right = jnp.where(odd_y, a, b), jnp.where(odd_y, b, a)
        for i in range(count):
            ahead, behind = turn(right, -room * i, 1), turn(left, 128 - width - room * i, 1)
            yield start + i, jnp.where(lane < width, ahead, jnp.where(lane >= 128 - width, behind, 0.0))


def weights_kernel(
    k_rows, ya, yb, k_hbm, k1_hbm, weights, inverse, diagonal, k1, w1, inverse1, diagonal1, k_out, wide, thin, sems,
):
    copies = Copies(sems)
    for q, outer in outer_columns(PACKED_K, KY, ya, yb):
        k_out[q, :, 0:128] = k_rows[q]
        k_out[q, :, 128:256] = outer
    flying = [copies.start(k_out.at[pl.ds(4, 14)], k_hbm)]
    for m in range(10):
        wide[m] = k_out[2 * m + 1] + k_out[2 * m + 2]
    thin[...] = dot(wide[...].reshape(10 * 64, 256), coarsen_matrix(256, 128, 140, 12, 0.125))
    for m in range(10):
        k1[m] = thin[pl.ds(64 * m, 32, stride=2), :] + thin[pl.ds(64 * m + 1, 32, stride=2), :]
    flying.append(copies.start(k1, k1_hbm))
    Level(k_out, weights, None, None, None, 1.0, *SHAPE0).set_up(1, 21, None, diagonal, inverse)
    Level(k1, w1, None, None, None, 0.25, *SHAPE1).set_up(1, 9, None, diagonal1, inverse1)
    for copy in flying:
        copy.wait()


def first_kernel(
    count, b_rows, ya, yb, weights, inverse, diagonal, k1, w1, inverse1, diagonal1,
    bh_hbm, x_hbm, b1_hbm, x1_hbm, sa_hbm, sb_hbm, g_hbm,
    bh, x_out, b1, bh1, x1, sa, sb, fine, wide, thin, fine1, thin1, g_out, sems,
):
    odd_x = odd("gx")
    copies = Copies(sems)
    for n, outer in outer_columns(PACKED_B, BY, ya, yb):
        q = n + 1
        bh[q, :, 0:128] = b_rows[n] * inverse[q, :, 0:128]
        bh[q, :, 128:256] = outer * inverse[q, :, 128:256]
    flying = []
    level = Level(None, weights, bh, x_out, None, 1.0, *SHAPE0)
    level.pre(2, 20)
    level.residue(3, 19, diagonal, fine, 0)
    for m in range(8):
        wide[m] = fine[2 * m] + fine[2 * m + 1]
    thin[...] = dot(wide[...].reshape(8 * 64, 256), coarsen_matrix(256, 128, 140, 12, 0.125))
    for m in range(8):
        b1[1 + m] = thin[pl.ds(64 * m, 32, stride=2), :] + thin[pl.ds(64 * m + 1, 32, stride=2), :]
        bh1[1 + m] = b1[1 + m] * inverse1[1 + m]
    flying.append(copies.start(bh.at[pl.ds(5, 12)], bh_hbm))
    flying.append(copies.start(x_out.at[pl.ds(4, 14)], x_hbm))
    flying.append(copies.start(b1, b1_hbm))

    level = Level(None, w1, bh1, x1, None, 0.25, *SHAPE1)
    level.pre(2, 8)
    taken = ((x1, 3, 4), (x1, 4, 5), (x1, 5, 6), (b1, 4, 5), (k1, 3, 6))
    pack_outer([jnp.where(odd_x, ref[to_left], ref[to_right]) for ref, to_right, to_left in taken], sa)
    pack_outer([jnp.where(odd_x, ref[to_right], ref[to_left]) for ref, to_right, to_left in taken], sb)
    level.residue(3, 7, diagonal1, fine1, 0)
    parts = [fine1[0] + fine1[1], fine1[2] + fine1[3], k1[3] + k1[4], k1[5] + k1[6]]
    thin1[...] = dot(jnp.concatenate(parts, axis=0), coarsen_matrix(128, 128, 64, 0, 0.125))
    payload = jnp.zeros((16, 128), F32)
    for n in range(4):
        part = thin1[pl.ds(32 * n, 16, stride=2), :] + thin1[pl.ds(32 * n + 1, 16, stride=2), :]
        payload = payload + turn(part, 32 * n, 1)
    for n in range(count):
        g_out[n] = payload
    flying += pieces(PIECES, g_out, g_hbm, copies)
    flying += [copies.start(*pair) for pair in ((x1, x1_hbm), (sa, sa_hbm), (sb, sb_hbm))]
    for copy in flying:
        copy.wait()


def pack_outer(rows_in, out):
    lane = iota((32, 128), 1)
    out[0] = jnp.where(lane < 64, rows_in[0], turn(rows_in[1], 64, 1))
    out[1] = jnp.where(lane < 64, rows_in[2], turn(rows_in[3], 64, 1))
    last = rows_in[4]
    for n, row in enumerate(rows_in):
        at = 64 + 12 * n
        last = jnp.where((lane >= at) & (lane < at + 6), turn(row, 12 * n, 1), last)
        last = jnp.where((lane >= at + 6) & (lane < at + 12), turn(row, 12 * n - 52, 1), last)
    out[2] = last


def unpack_outer(tiles, n):
    lane = iota((32, 128), 1)
    own = turn(tiles[n // 2], 64 * (n % 2), 1)
    right, left = turn(tiles[2], -12 * n, 1), turn(tiles[2], 52 - 12 * n, 1)
    return jnp.where(lane < 64, own, jnp.where(lane < 70, right, jnp.where(lane >= 122, left, 0.0)))


def prepare_kernel(
    ra_hbm, rb_hbm, k1_hbm, b1_hbm, x1_hbm, k_hbm, bh_hbm, x_hbm, w0, bh0, d0, x0, w1, bh1, x1,
    ra, rb, k1_in, b1_in, x1_in, k0, k1, b1, sems,
):
    odd_x = odd("gx")
    copies = Copies(sems)
    for_level0 = [copies.start(k_hbm, k0), copies.start(bh_hbm, bh0.at[pl.ds(1, 12)]), copies.start(x_hbm, x0)]
    for_level1 = [copies.start(*pair) for pair in ((ra_hbm, ra), (rb_hbm, rb), (k1_hbm, k1_in), (b1_hbm, b1_in), (x1_hbm, x1_in))]
    for copy in for_level1:
        copy.wait()
    for side in range(2):
        tiles = [jnp.where(odd_x, ra[n], rb[n]) if side == 0 else jnp.where(odd_x, rb[n], ra[n]) for n in range(3)]
        for n in range(3):
            x1[n if side == 0 else 9 + n] = unpack_outer(tiles, n)
        b1[1 if side == 0 else 10] = unpack_outer(tiles, 3)
        k1[0 if side == 0 else 11] = unpack_outer(tiles, 4)
    for n in range(6):
        x1[3 + n] = x1_in[2 + n]
    for n in range(8):
        b1[2 + n] = b1_in[1 + n]
    for n in range(10):
        k1[1 + n] = k1_in[n]
    Level(k1, w1, bh1, None, None, 0.25, *SHAPE1).set_up(1, 11, b1)
    for copy in for_level0:
        copy.wait()
    Level(k0, w0, None, None, None, 1.0, *SHAPE0).set_up(1, 13, None, d0)


def window_start(me, count, window):
    return jnp.clip(me - WINDOW // 2, 0, count - window)


def last_kernel(
    count, w0, bh0, d0, x0, w1, bh1, x1, g, ga, gb, pressure, residual,
    k2, b2, w2, bh2, x2, y2, p2, fine2, sums2, coarse2, t1, y1, p1, stack1, t0, y0, p0, stack0, pressure_rows, residual_rows, sems,
):
    copies = Copies(sems)
    odd_y = odd("gy")
    me = lax.axis_index("gx")
    lane = iota((16, 128), 1)

    start = window_start(me, count, g.shape[0])

    def window(j, carry):
        device = me - WINDOW // 2 + j
        inside = (device >= 0) & (device < count)
        at = jnp.clip(device - start, 0, g.shape[0] - 1)
        own, a, b = g[at], ga[at], gb[at]
        left, right = jnp.where(odd_y, a, b), jnp.where(odd_y, b, a)
        for n, out in ((0, b2), (2, k2)):
            for m in range(2):
                s = -32 * (n + m)
                value = jnp.where(lane < 32, turn(own, s, 1), jnp.where(lane < 64, turn(right, s + 32, 1), jnp.where(lane >= 96, turn(left, s + 96, 1), 0.0)))
                out[2 * j + m] = jnp.where(inside, value, 0.0)
        return carry

    lax.fori_loop(0, WINDOW, window, 0, unroll=WINDOW_UNROLL)
    level = Level(k2, w2, bh2, x2, p2, 0.0625, *SHAPE2)
    level.set_up(1, 45, b2, y2)
    level.pre(2, 44)
    level.residue(4, 42, y2, fine2, 4)
    zero = jnp.zeros((16, 128), F32)
    for m in (0, 1, 21, 22):
        sums2[m] = zero
    for m in range(2, 21):
        sums2[m] = fine2[2 * m] + fine2[2 * m + 1]
    for m in range(23):
        sums2[23 + m] = k2[2 * m] + k2[2 * m + 1]
    coarse2[...] = dot(sums2[...].reshape(46 * 16, 128), coarsen_matrix(128, 128, 64, 32, 0.125))
    both = coarse2[pl.ds(0, 46 * 8, stride=2), :] + coarse2[pl.ds(1, 46 * 8, stride=2), :]
    both = both.reshape(46, 8, 128)
    b3, k3 = both[:23], both[23:]
    none = jnp.zeros((1, 8, 128), F32)

    def after(value):
        return jnp.concatenate([value[1:], none], axis=0)

    def before(value):
        return jnp.concatenate([none, value[:-1]], axis=0)

    w3, inverse, _ = weights_row(k3, before(k3), after(k3), 0.015625)
    middle, steps = chebyshev(COARSE, COARSE_LOW)
    source = b3 * inverse
    update = source * (1 / middle)
    e3 = update
    for c1, c2 in steps:
        update = c1 * update + c2 * (source - e3 + neighbour_sum(w3, before(e3), e3, after(e3)))
        e3 = e3 + update

    tall = coarse2
    for m in range(5):
        for half in range(2):
            tall[pl.ds(16 * m + half, 8, stride=2), :] = e3[9 + m]
    fine = dot(tall[0 : 5 * 16, :], refine_matrix(128, 128, 64, 32))
    for m in range(10):
        part = fine[16 * (m // 2) : 16 * (m // 2) + 16]
        x2[18 + m] = x2[18 + m] + part
    level.post(20, 26, y2)

    for m in range(6):
        for half in range(2):
            stack1[pl.ds(32 * m + half, 16, stride=2), :] = x2[20 + m]
    fine = dot(stack1[...], refine_matrix(128, 128, 70, 6))
    for m in range(12):
        t1[m] = x1[m] + fine[32 * (m // 2) : 32 * (m // 2) + 32]
    level = Level(None, w1, bh1, t1, p1, 0.25, *SHAPE1)
    level.post(2, 10, y1)

    for m in range(8):
        for half in range(2):
            stack0[pl.ds(64 * m + half, 32, stride=2), :] = t1[2 + m]
    matrix = refine_matrix(128, 256, 140, 12)
    fine = dot(stack0[...], matrix)
    for m in range(14):
        row = (m + 1) // 2
        t0[m] = x0[m] + fine[64 * row : 64 * row + 64]
    level = Level(None, w0, bh0, t0, p0, 1.0, *SHAPE0)
    level.post(2, 12, y0)
    for i in range(8):
        pressure_rows[pl.ds(i, 64, stride=8), :] = t0[3 + i, :, 0:128]
    waits = pieces(PIECES, pressure_rows, pressure, copies)
    for i in range(8):
        q = 3 + i
        value = d0[q] * (bh0[q] - t0[q] + level.total(t0, q, q - 1, q + 1))
        residual_rows[pl.ds(i, 64, stride=8), :] = value[:, 0:128]
    waits += pieces(PIECES, residual_rows, residual, copies)
    for copy in waits:
        copy.wait()


def on_device(right_side, conductivity):
    count = lax.axis_size("gx")
    b, k = right_side.reshape(512, 128), conductivity.reshape(512, 128)
    plane = (64, 128)

    def strips(value, width):
        own, xa, xb = call(
            functools.partial(strip_kernel, width),
            [(8,) + plane] + [(width,) + plane] * 2,
            [(512, 128)],
            value,
            hbm_in=1,
            sems=[(PIECES,)],
        )
        return own, swap(xa, "gx", 0), swap(xb, "gx", 1)

    own_k, xka, xkb = strips(k, KX)
    own_b, xba, xbb = strips(b, BX)

    def packed(own, xa, xb, pack, width):
        rows_out, ya, yb = call(
            functools.partial(pack_kernel, pack, width),
            [(8 + 2 * xa.shape[0],) + plane] + [(len(pack),) + plane] * 2,
            [],
            own, xa, xb,
            cost=pl.CostEstimate(flops=1_000_000, bytes_accessed=2_000_000, transcendentals=0),
        )
        return rows_out, swap(ya, "gy", 0), swap(yb, "gy", 1)

    rows0, rows1, rows2, rows3 = (22, 64, 256), (10, 32, 128), (46, 16, 128), (12, 32, 128)
    wide0 = (14, 64, 256)
    k0, k1, *about_k = call(
        weights_kernel,
        [wide0, rows1, (6,) + rows0, rows0, rows0, rows1, (6,) + rows1, rows1, rows1],
        [rows0, (10, 64, 256), (10 * 64, 128)],
        *packed(own_k, xka, xkb, PACKED_K, KY),
        hbm_out=2,
        sems=[(2,)],
        cost=pl.CostEstimate(flops=20_000_000, bytes_accessed=8_000_000, transcendentals=300_000),
    )
    bh0, x0, b1, x1, sa, sb, g = call(
        functools.partial(first_kernel, count),
        [(12, 64, 256), wide0, rows1, rows1, (3, 32, 128), (3, 32, 128), (count, 16, 128)],
        [rows0, rows0, rows1, rows1, rows1, (3, 32, 128), (3, 32, 128)]
        + [(16, 64, 256), (8, 64, 256), (8 * 64, 128), (4, 32, 128), (128, 128), (count, 16, 128)],
        *packed(own_b, xba, xbb, PACKED_B, BY), *about_k,
        hbm_out=7,
        sems=[(6 + PIECES,)],
    )
    ra, rb = swap(sa, "gx", 0), swap(sb, "gx", 1)
    g = lax.all_to_all(g, "gx", 0, 0, tiled=True)
    g, ra, rb, k0, bh0, x0, k1, b1, x1 = lax.optimization_barrier((g, ra, rb, k0, bh0, x0, k1, b1, x1))
    window = min(WINDOW, count)
    g = lax.dynamic_slice_in_dim(g, window_start(lax.axis_index("gx"), count, window), window)
    ga, gb = swap(g, "gy", 0), swap(g, "gy", 1)
    kept = call(
        prepare_kernel,
        [(6,) + wide0, wide0, wide0, wide0, (6,) + rows3, rows3, rows3],
        [(3, 32, 128), (3, 32, 128), rows1, rows1, rows1, wide0, rows3, rows3],
        ra, rb, k1, b1, x1, k0, bh0, x0,
        hbm_in=8,
        sems=[(8,)],
        cost=pl.CostEstimate(flops=20_000_000, bytes_accessed=8_000_000, transcendentals=200_000),
    )
    pressure, residual = call(
        functools.partial(last_kernel, count),
        [(512, 128)] * 2,
        [rows2, rows2, (6,) + rows2, rows2, rows2, rows2, rows2, rows2, rows2, (46 * 16, 128)]
        + [rows3, rows3, rows3, (6 * 32, 128)]
        + [wide0, wide0, wide0, (8 * 64, 128), (512, 128), (512, 128)],
        *kept, g, ga, gb,
        hbm_out=2,
        sems=[(2 * PIECES,)],
    )
    return pressure.reshape(64, 8, 128), residual.reshape(64, 8, 128)


def solution(mesh):
    place = P(None, "gx", "gy")
    return jax.shard_map(
        on_device, mesh=mesh, in_specs=(place, place), out_specs=(place, place), check_vma=False
    )
```

```python
import functools

import jax
import jax.numpy as jnp
from jax import lax
from jax.experimental import pallas as pl
from jax.experimental.pallas import tpu as pltpu
from jax.sharding import PartitionSpec as P

F32 = jnp.float32
COARSE = 8
LOW_BOUND = 0.3
HIGH_BOUND = 2.0
COARSE_LOW = 0.02
VMEM_LIMIT = 28 * 1024 * 1024

SHAPE0, SHAPE1, SHAPE2, WINDOW_UNROLL = (1, True), (4, True), (4, True), True

WINDOW = 23

PIECES = 4

KX, BX, KY, BY = 7, 6, 13, 12
PACKED_K = ((0, 9), (9, 9), (18, 4))
PACKED_B = ((0, 10), (10, 10))


def pairs(size, offset):
    found = []
    for i in range(offset, size - 1, 2):
        found += [(i, i + 1), (i + 1, i)]
    return found


def swap(value, axis, offset):
    return lax.ppermute(value, axis, pairs(lax.axis_size(axis), offset))


def chebyshev(sweeps, lower):
    middle = (HIGH_BOUND + lower) / 2
    half_width = (HIGH_BOUND - lower) / 2
    ratio = middle / half_width
    rho = 1 / ratio
    steps = []
    for _ in range(sweeps - 1):
        rho_next = 1 / (2 * ratio - rho)
        steps.append((rho_next * rho, 2 * rho_next / half_width))
        rho = rho_next
    return middle, steps


def iota(shape, axis):
    return lax.broadcasted_iota(jnp.int32, shape, axis)


def dot(a, b):
    b = b.astype(jnp.bfloat16)
    total = None
    for _ in range(3):
        piece = a.astype(jnp.bfloat16)
        a = a - piece.astype(F32)
        part = jnp.dot(piece, b, preferred_element_type=F32)
        total = part if total is None else total + part
    return total


def coarsen_matrix(fine, coarse, right, left, scale):
    f, c = iota((fine, coarse), 0), iota((fine, coarse), 1)
    ahead = (f < right) & (c == lax.shift_right_logical(f, 1))
    behind = (f >= fine - left) & (coarse - c == lax.shift_right_logical(fine - f + 1, 1))
    return jnp.where(ahead | behind, scale, 0.0).astype(F32)


def refine_matrix(coarse, fine, right, left):
    c, f = iota((coarse, fine), 0), iota((coarse, fine), 1)
    ahead = (f < right) & (c == lax.shift_right_logical(f, 1))
    behind = (f >= fine - left) & (coarse - c == lax.shift_right_logical(fine - f + 1, 1))
    return jnp.where(ahead | behind, 1.0, 0.0).astype(F32)


def turn(value, shift, axis):
    shift = shift % value.shape[axis]
    return value if shift == 0 else pltpu.roll(value, shift, axis=axis)


def edged(value, axis, top):
    depth = value.shape[axis]
    cut = functools.partial(lax.slice_in_dim, value, axis=axis)
    index = iota(value.shape[:axis] + (8,) + value.shape[axis + 1 :], axis)
    if top:
        edge = jnp.where(index == 7, 0.0, cut(depth - 8, depth))
        return edge if depth == 8 else jnp.concatenate([cut(0, depth - 8), edge], axis=axis)
    edge = jnp.where(index == 0, 0.0, cut(0, 8))
    return edge if depth == 8 else jnp.concatenate([edge, cut(8, depth)], axis=axis)


def weights_row(kc, km, kp, factor):
    axis = kc.ndim - 2
    up = kc + edged(turn(kc, -1, axis), axis, True)
    down = kc + edged(turn(kc, 1, axis), axis, False)
    ahead = kc + turn(kc, -1, axis + 1)
    behind = kc + turn(kc, 1, axis + 1)
    right = kc + kp
    left = kc + km
    diagonal = (up + down) + (ahead + behind) + (right + left)
    inverse = jnp.where(kc > 0, 1.0 / diagonal, 0.0)
    weights = [w * inverse for w in (left, right, behind, ahead, edged(down, axis, False), edged(up, axis, True))]
    return weights, inverse * (2.0 / factor), diagonal * (0.5 * factor)


def neighbour_sum(weights, below, centre, above):
    axis = centre.ndim - 2
    left, right, behind, ahead, down, up = weights
    total = left * below + right * above
    total = total + behind * turn(centre, 1, axis + 1) + ahead * turn(centre, -1, axis + 1)
    return total + down * turn(centre, 1, axis) + up * turn(centre, -1, axis)


def rows(low, high, body, chunk, unroll):
    full = (high - low) // chunk

    def step(n, carry):
        body(pl.ds(low + n * chunk, chunk), pl.ds(low + n * chunk - 1, chunk), pl.ds(low + n * chunk + 1, chunk))
        return carry

    lax.fori_loop(0, full, step, 0, unroll=unroll)
    at = low + full * chunk
    if at < high:
        body(pl.ds(at, high - at), pl.ds(at - 1, high - at), pl.ds(at + 1, high - at))


class Level:
    def __init__(self, k, weights, bh, x, p, factor, chunk, unroll):
        self.k, self.weights, self.bh, self.x, self.p, self.factor = k, weights, bh, x, p, factor
        self.chunk, self.unroll = chunk, unroll

    def rows(self, low, high, body):
        rows(low, high, body, self.chunk, self.unroll)

    def set_up(self, low, high, b=None, diagonal=None, inverses=None):
        def body(q, below, above):
            weights, inverse, diag = weights_row(self.k[q], self.k[below], self.k[above], self.factor)
            for n in range(6):
                self.weights[n, q] = weights[n]
            if b is not None:
                self.bh[q] = b[q] * inverse
            if inverses is not None:
                inverses[q] = inverse
            if diagonal is not None:
                diagonal[q] = diag

        self.rows(low, high, body)

    def total(self, x, q, below, above):
        return neighbour_sum([self.weights[n, q] for n in range(6)], x[below], x[q], x[above])

    def pre(self, low, high):
        middle, ((c1, c2),) = chebyshev(2, LOW_BOUND)

        def body(q, below, above):
            first = self.bh[q]
            total = self.total(self.bh, q, below, above)
            self.x[q] = (1 / middle) * (1 + c1 - c2 + c2 * middle) * first + (c2 / middle) * total

        self.rows(low, high, body)

    def residue(self, low, high, diagonal, out, at):
        def body(q, below, above):
            value = diagonal[q] * (self.bh[q] - self.x[q] + self.total(self.x, q, below, above))
            out[pl.ds(q.start + (at - low), q.size)] = value

        self.rows(low, high, body)

    def post(self, low, high, out):
        middle, ((c1, c2),) = chebyshev(2, LOW_BOUND)

        def first(q, below, above):
            update = (self.bh[q] - self.x[q] + self.total(self.x, q, below, above)) * (1 / middle)
            self.p[q] = update
            out[q] = self.x[q] + update

        def second(q, below, above):
            residue = self.bh[q] - out[q] + self.total(out, q, below, above)
            self.x[q] = out[q] + c1 * self.p[q] + c2 * residue

        self.rows(low - 1, high + 1, first)
        self.rows(low, high, second)


def spec(n):
    return [pl.BlockSpec(memory_space=pltpu.VMEM)] * n


def call(body, outs, scratch, *args, hbm_in=0, hbm_out=0, sems=(), cost=None):
    args = [pltpu.with_memory_space_constraint(x, pltpu.HBM) if n < hbm_in else x for n, x in enumerate(args)]
    return pl.pallas_call(
        body,
        out_shape=[pltpu.HBM(s, F32) if n < hbm_out else jax.ShapeDtypeStruct(s, F32) for n, s in enumerate(outs)],
        in_specs=[pl.BlockSpec(memory_space=pltpu.HBM)] * hbm_in + spec(len(args) - hbm_in),
        out_specs=[pl.BlockSpec(memory_space=pltpu.HBM)] * hbm_out + spec(len(outs) - hbm_out),
        scratch_shapes=[pltpu.VMEM(s, F32) for s in scratch] + [pltpu.SemaphoreType.DMA(s) for s in sems],
        compiler_params=pltpu.CompilerParams(vmem_limit_bytes=VMEM_LIMIT),
        cost_estimate=cost,
    )(*args)


class Copies:
    def __init__(self, sems):
        self.sems, self.used = sems, 0

    def start(self, source, target):
        copy = pltpu.make_async_copy(source, target, self.sems.at[self.used])
        copy.start()
        self.used += 1
        return copy


def odd(axis):
    return lax.rem(lax.axis_index(axis), 2) == 1


def pieces(n, source, target, copies):
    size = source.shape[0] // n
    return [copies.start(source.at[pl.ds(i * size, size)], target.at[pl.ds(i * size, size)]) for i in range(n)]


def strip_kernel(width, source, own, xa, xb, ref, sems):
    odd_x = odd("gx")
    depth = 64 // PIECES
    for n, copy in enumerate(pieces(PIECES, source, ref, Copies(sems))):
        copy.wait()
        z = pl.ds(depth * n, depth)
        planes = [ref[pl.ds(8 * depth * n + i, depth, stride=8), :] for i in range(8)]
        for i in range(8):
            own[i, z] = planes[i]
        for i in range(width):
            first, last = planes[i], planes[8 - width + i]
            xa[i, z] = jnp.where(odd_x, first, last)
            xb[i, z] = jnp.where(odd_x, last, first)


def pack_kernel(packed, width, own, xa, xb, rows_out, ya, yb):
    odd_x, odd_y = odd("gx"), odd("gy")
    lane = iota((64, 128), 1)
    halo = xa.shape[0]
    planes = [None] * (8 + 2 * halo)
    for n in range(halo):
        a, b = xa[n], xb[n]
        planes[n], planes[8 + halo + n] = jnp.where(odd_x, a, b), jnp.where(odd_x, b, a)
    for i in range(8):
        planes[halo + i] = own[i]
    for n, plane in enumerate(planes):
        rows_out[n] = plane
    for n, (start, count) in enumerate(packed):
        first, last = jnp.zeros((64, 128), F32), jnp.zeros((64, 128), F32)
        for i in range(count + 1):
            this, before = planes[start + min(i, count - 1)], planes[start + max(i - 1, 0)]
            turned = turn(jnp.where(lane < 64, this, before), width * i, 1)
            if i < count:
                first = jnp.where((lane >= width * i) & (lane < width * (i + 1)), turned, first)
            if i > 0:
                last = jnp.where((lane >= width * (i - 1)) & (lane < width * i), turned, last)
        ya[n] = jnp.where(odd_y, first, last)
        yb[n] = jnp.where(odd_y, last, first)


def outer_columns(packed, width, ya, yb):
    odd_y = odd("gy")
    lane = iota((64, 128), 1)
    for n, (start, count) in enumerate(packed):
        a, b = ya[n], yb[n]
        left, right = jnp.where(odd_y, a, b), jnp.where(odd_y, b, a)
        ahead = right
        for i in range(count):
            behind = turn(jnp.where(lane < width * (i + 1), left, right), -width * (i + 1), 1)
            yield start + i, jnp.where(lane < width, ahead, jnp.where(lane >= 128 - width, behind, 0.0))
            ahead = behind


def weights_kernel(
    k_rows, ya, yb, k_hbm, k1_hbm, weights, inverse, diagonal, k1, w1, inverse1, diagonal1, k_out, wide, thin, sems,
):
    copies = Copies(sems)
    for q, outer in outer_columns(PACKED_K, KY, ya, yb):
        k_out[q, :, 0:128] = k_rows[q]
        k_out[q, :, 128:256] = outer
    for m in range(10):
        wide[m] = k_out[2 * m + 1] + k_out[2 * m + 2]
    thin[...] = dot(wide[...].reshape(10 * 64, 256), coarsen_matrix(256, 128, 140, 12, 0.125))
    for m in range(10):
        k1[m] = thin[pl.ds(64 * m, 32, stride=2), :] + thin[pl.ds(64 * m + 1, 32, stride=2), :]
    flying = [copies.start(k_out.at[pl.ds(4, 14)], k_hbm), copies.start(k1, k1_hbm)]
    Level(k_out, weights, None, None, None, 1.0, *SHAPE0).set_up(1, 21, None, diagonal, inverse)
    Level(k1, w1, None, None, None, 0.25, *SHAPE1).set_up(1, 9, None, diagonal1, inverse1)
    for copy in flying:
        copy.wait()


def first_kernel(
    count, b_rows, ya, yb, weights, inverse, diagonal, k1, w1, inverse1, diagonal1,
    bh_hbm, x_hbm, b1_hbm, x1_hbm, sa_hbm, sb_hbm, g_hbm,
    bh, x_out, b1, bh1, x1, sa, sb, fine, wide, thin, fine1, thin1, g_out, sems,
):
    odd_x = odd("gx")
    copies = Copies(sems)
    for n, outer in outer_columns(PACKED_B, BY, ya, yb):
        q = n + 1
        bh[q, :, 0:128] = b_rows[n] * inverse[q, :, 0:128]
        bh[q, :, 128:256] = outer * inverse[q, :, 128:256]
    flying = []
    level = Level(None, weights, bh, x_out, None, 1.0, *SHAPE0)
    level.pre(2, 20)
    level.residue(3, 19, diagonal, fine, 0)
    for m in range(8):
        wide[m] = fine[2 * m] + fine[2 * m + 1]
    thin[...] = dot(wide[...].reshape(8 * 64, 256), coarsen_matrix(256, 128, 140, 12, 0.125))
    for m in range(8):
        b1[1 + m] = thin[pl.ds(64 * m, 32, stride=2), :] + thin[pl.ds(64 * m + 1, 32, stride=2), :]
        bh1[1 + m] = b1[1 + m] * inverse1[1 + m]
    flying.append(copies.start(bh.at[pl.ds(5, 12)], bh_hbm))
    flying.append(copies.start(x_out.at[pl.ds(4, 14)], x_hbm))
    flying.append(copies.start(b1, b1_hbm))

    level = Level(None, w1, bh1, x1, None, 0.25, *SHAPE1)
    level.pre(2, 8)
    taken = ((x1, 3, 4), (x1, 4, 5), (x1, 5, 6), (b1, 4, 5), (k1, 3, 6))
    pack_outer([jnp.where(odd_x, ref[to_left], ref[to_right]) for ref, to_right, to_left in taken], sa)
    pack_outer([jnp.where(odd_x, ref[to_right], ref[to_left]) for ref, to_right, to_left in taken], sb)
    level.residue(3, 7, diagonal1, fine1, 0)
    parts = [fine1[0] + fine1[1], fine1[2] + fine1[3], k1[3] + k1[4], k1[5] + k1[6]]
    thin1[...] = dot(jnp.concatenate(parts, axis=0), coarsen_matrix(128, 128, 64, 0, 0.125))
    payload = jnp.zeros((16, 128), F32)
    for n in range(4):
        part = thin1[pl.ds(32 * n, 16, stride=2), :] + thin1[pl.ds(32 * n + 1, 16, stride=2), :]
        payload = payload + turn(part, 32 * n, 1)
    for n in range(count):
        g_out[n] = payload
    flying += pieces(PIECES, g_out, g_hbm, copies)
    flying += [copies.start(*pair) for pair in ((x1, x1_hbm), (sa, sa_hbm), (sb, sb_hbm))]
    for copy in flying:
        copy.wait()


def pack_outer(rows_in, out):
    lane = iota((32, 128), 1)
    out[0] = jnp.where(lane < 64, rows_in[0], turn(rows_in[1], 64, 1))
    out[1] = jnp.where(lane < 64, rows_in[2], turn(rows_in[3], 64, 1))
    last = rows_in[4]
    for n, row in enumerate(rows_in):
        at = 64 + 12 * n
        last = jnp.where((lane >= at) & (lane < at + 6), turn(row, 12 * n, 1), last)
        last = jnp.where((lane >= at + 6) & (lane < at + 12), turn(row, 12 * n - 52, 1), last)
    out[2] = last


def unpack_outer(tiles, n):
    lane = iota((32, 128), 1)
    own = turn(tiles[n // 2], 64 * (n % 2), 1)
    right, left = turn(tiles[2], -12 * n, 1), turn(tiles[2], 52 - 12 * n, 1)
    return jnp.where(lane < 64, own, jnp.where(lane < 70, right, jnp.where(lane >= 122, left, 0.0)))


def prepare_kernel(
    ra_hbm, rb_hbm, k1_hbm, b1_hbm, x1_hbm, k_hbm, bh_hbm, x_hbm, w0, bh0, d0, x0, w1, bh1, x1,
    ra, rb, k1_in, b1_in, x1_in, k0, k1, b1, sems,
):
    odd_x = odd("gx")
    copies = Copies(sems)
    for_level0 = [copies.start(k_hbm, k0), copies.start(bh_hbm, bh0.at[pl.ds(1, 12)]), copies.start(x_hbm, x0)]
    for_level1 = [copies.start(*pair) for pair in ((ra_hbm, ra), (rb_hbm, rb), (k1_hbm, k1_in), (b1_hbm, b1_in), (x1_hbm, x1_in))]
    for copy in for_level1:
        copy.wait()
    for side in range(2):
        tiles = [jnp.where(odd_x, ra[n], rb[n]) if side == 0 else jnp.where(odd_x, rb[n], ra[n]) for n in range(3)]
        for n in range(3):
            x1[n if side == 0 else 9 + n] = unpack_outer(tiles, n)
        b1[1 if side == 0 else 10] = unpack_outer(tiles, 3)
        k1[0 if side == 0 else 11] = unpack_outer(tiles, 4)
    for n in range(6):
        x1[3 + n] = x1_in[2 + n]
    for n in range(8):
        b1[2 + n] = b1_in[1 + n]
    for n in range(10):
        k1[1 + n] = k1_in[n]
    Level(k1, w1, bh1, None, None, 0.25, *SHAPE1).set_up(1, 11, b1)
    for copy in for_level0:
        copy.wait()
    Level(k0, w0, None, None, None, 1.0, *SHAPE0).set_up(1, 13, None, d0)


def window_start(me, count, window):
    return jnp.clip(me - WINDOW // 2, 0, count - window)


def last_kernel(
    count, w0, bh0, d0, x0, w1, bh1, x1, g, ga, gb, pressure, residual,
    k2, b2, w2, bh2, x2, y2, p2, fine2, sums2, coarse2, t1, y1, p1, stack1, t0, y0, p0, stack0, pressure_rows, residual_rows, sems,
):
    copies = Copies(sems)
    odd_y = odd("gy")
    me = lax.axis_index("gx")
    lane = iota((16, 128), 1)

    start = window_start(me, count, g.shape[0])

    def window(j, carry):
        device = me - WINDOW // 2 + j
        inside = (device >= 0) & (device < count)
        at = jnp.clip(device - start, 0, g.shape[0] - 1)
        own, a, b = g[at], ga[at], gb[at]
        left, right = jnp.where(odd_y, a, b), jnp.where(odd_y, b, a)
        by32 = turn(jnp.where(lane < 32, left, jnp.where(lane < 64, own, right)), -32, 1)
        by64 = turn(jnp.where(lane < 64, left, jnp.where(lane < 96, own, right)), -64, 1)
        by96 = turn(jnp.where(lane < 32, right, jnp.where(lane < 96, left, own)), -96, 1)
        for out, m, parts in ((b2, 0, (own, by96, by32)), (b2, 1, (by32, right, by64)), (k2, 0, (by64, by32, by96)), (k2, 1, (by96, by64, left))):
            value = jnp.where(lane < 32, parts[0], jnp.where(lane < 64, parts[1], jnp.where(lane >= 96, parts[2], 0.0)))
            out[2 * j + m] = jnp.where(inside, value, 0.0) if out is k2 else value
        return carry

    lax.fori_loop(0, WINDOW, window, 0, unroll=WINDOW_UNROLL)
    level = Level(k2, w2, bh2, x2, p2, 0.0625, *SHAPE2)
    level.set_up(1, 45, b2, y2)
    level.pre(2, 44)
    level.residue(4, 42, y2, fine2, 4)
    zero = jnp.zeros((16, 128), F32)
    for m in (0, 1, 21, 22):
        sums2[m] = zero
    for m in range(2, 21):
        sums2[m] = fine2[2 * m] + fine2[2 * m + 1]
    for m in range(23):
        sums2[23 + m] = k2[2 * m] + k2[2 * m + 1]
    coarse2[...] = dot(sums2[...].reshape(46 * 16, 128), coarsen_matrix(128, 128, 64, 32, 0.125))
    both = coarse2[pl.ds(0, 46 * 8, stride=2), :] + coarse2[pl.ds(1, 46 * 8, stride=2), :]
    both = both.reshape(46, 8, 128)
    b3, k3 = both[:23], both[23:]
    w3, inverse, _ = weights_row(k3[2:21], k3[1:20], k3[3:22], 0.015625)
    middle, steps = chebyshev(COARSE, COARSE_LOW)
    source = b3[2:21] * inverse
    update = source * (1 / middle)
    e3 = update
    for n, (c1, c2) in enumerate(steps):
        inner = slice(n + 1, 18 - n)
        below, centre, above = e3[:-2], e3[1:-1], e3[2:]
        total = neighbour_sum([w[inner] for w in w3], below, centre, above)
        update = c1 * update[1:-1] + c2 * (source[inner] - centre + total)
        e3 = centre + update

    tall = coarse2
    for m in range(5):
        for half in range(2):
            tall[pl.ds(16 * m + half, 8, stride=2), :] = e3[m]
    fine = dot(tall[0 : 5 * 16, :], refine_matrix(128, 128, 64, 32))
    for m in range(10):
        part = fine[16 * (m // 2) : 16 * (m // 2) + 16]
        x2[18 + m] = x2[18 + m] + part
    level.post(20, 26, y2)

    for m in range(6):
        for half in range(2):
            stack1[pl.ds(32 * m + half, 16, stride=2), :] = x2[20 + m]
    fine = dot(stack1[...], refine_matrix(128, 128, 70, 6))
    for m in range(12):
        t1[m] = x1[m] + fine[32 * (m // 2) : 32 * (m // 2) + 32]
    level = Level(None, w1, bh1, t1, p1, 0.25, *SHAPE1)
    level.post(2, 10, y1)

    for m in range(8):
        for half in range(2):
            stack0[pl.ds(64 * m + half, 32, stride=2), :] = t1[2 + m]
    matrix = refine_matrix(128, 256, 140, 12)
    fine = dot(stack0[...], matrix)
    for m in range(14):
        row = (m + 1) // 2
        t0[m] = x0[m] + fine[64 * row : 64 * row + 64]
    level = Level(None, w0, bh0, t0, p0, 1.0, *SHAPE0)
    level.post(2, 12, y0)
    for i in range(8):
        pressure_rows[pl.ds(i, 64, stride=8), :] = t0[3 + i, :, 0:128]
    waits = pieces(PIECES, pressure_rows, pressure, copies)
    for i in range(8):
        q = 3 + i
        value = d0[q] * (bh0[q] - t0[q] + level.total(t0, q, q - 1, q + 1))
        residual_rows[pl.ds(i, 64, stride=8), :] = value[:, 0:128]
    waits += pieces(PIECES, residual_rows, residual, copies)
    for copy in waits:
        copy.wait()


def on_device(right_side, conductivity):
    count = lax.axis_size("gx")
    b, k = right_side.reshape(512, 128), conductivity.reshape(512, 128)
    plane = (64, 128)

    def strips(value, width):
        own, xa, xb = call(
            functools.partial(strip_kernel, width),
            [(8,) + plane] + [(width,) + plane] * 2,
            [(512, 128)],
            value,
            hbm_in=1,
            sems=[(PIECES,)],
        )
        return own, swap(xa, "gx", 0), swap(xb, "gx", 1)

    own_k, xka, xkb = strips(k, KX)
    own_b, xba, xbb = strips(b, BX)

    def packed(own, xa, xb, pack, width):
        rows_out, ya, yb = call(
            functools.partial(pack_kernel, pack, width),
            [(8 + 2 * xa.shape[0],) + plane] + [(len(pack),) + plane] * 2,
            [],
            own, xa, xb,
            cost=pl.CostEstimate(flops=1_000_000, bytes_accessed=2_000_000, transcendentals=0),
        )
        return rows_out, swap(ya, "gy", 0), swap(yb, "gy", 1)

    rows0, rows1, rows2, rows3 = (22, 64, 256), (10, 32, 128), (46, 16, 128), (12, 32, 128)
    wide0 = (14, 64, 256)
    k0, k1, *about_k = call(
        weights_kernel,
        [wide0, rows1, (6,) + rows0, rows0, rows0, rows1, (6,) + rows1, rows1, rows1],
        [rows0, (10, 64, 256), (10 * 64, 128)],
        *packed(own_k, xka, xkb, PACKED_K, KY),
        hbm_out=2,
        sems=[(2,)],
        cost=pl.CostEstimate(flops=20_000_000, bytes_accessed=8_000_000, transcendentals=300_000),
    )
    bh0, x0, b1, x1, sa, sb, g = call(
        functools.partial(first_kernel, count),
        [(12, 64, 256), wide0, rows1, rows1, (3, 32, 128), (3, 32, 128), (count, 16, 128)],
        [rows0, rows0, rows1, rows1, rows1, (3, 32, 128), (3, 32, 128)]
        + [(16, 64, 256), (8, 64, 256), (8 * 64, 128), (4, 32, 128), (128, 128), (count, 16, 128)],
        *packed(own_b, xba, xbb, PACKED_B, BY), *about_k,
        hbm_out=7,
        sems=[(6 + PIECES,)],
    )
    ra, rb = swap(sa, "gx", 0), swap(sb, "gx", 1)
    g = lax.all_to_all(g, "gx", 0, 0, tiled=True)
    g, ra, rb, k0, bh0, x0, k1, b1, x1 = lax.optimization_barrier((g, ra, rb, k0, bh0, x0, k1, b1, x1))
    window = min(WINDOW, count)
    g = lax.dynamic_slice_in_dim(g, window_start(lax.axis_index("gx"), count, window), window)
    ga, gb = swap(g, "gy", 0), swap(g, "gy", 1)
    kept = call(
        prepare_kernel,
        [(6,) + wide0, wide0, wide0, wide0, (6,) + rows3, rows3, rows3],
        [(3, 32, 128), (3, 32, 128), rows1, rows1, rows1, wide0, rows3, rows3],
        ra, rb, k1, b1, x1, k0, bh0, x0,
        hbm_in=8,
        sems=[(8,)],
        cost=pl.CostEstimate(flops=20_000_000, bytes_accessed=8_000_000, transcendentals=200_000),
    )
    pressure, residual = call(
        functools.partial(last_kernel, count),
        [(512, 128)] * 2,
        [rows2, rows2, (6,) + rows2, rows2, rows2, rows2, rows2, rows2, rows2, (46 * 16, 128)]
        + [rows3, rows3, rows3, (6 * 32, 128)]
        + [wide0, wide0, wide0, (8 * 64, 128), (512, 128), (512, 128)],
        *kept, g, ga, gb,
        hbm_out=2,
        sems=[(2 * PIECES,)],
    )
    return pressure.reshape(64, 8, 128), residual.reshape(64, 8, 128)


def solution(mesh):
    place = P(None, "gx", "gy")
    return jax.shard_map(
        on_device, mesh=mesh, in_specs=(place, place), out_specs=(place, place), check_vma=False
    )
```

```python
import functools

import jax
import jax.numpy as jnp
from jax import lax
from jax.experimental import pallas as pl
from jax.experimental.pallas import tpu as pltpu
from jax.sharding import PartitionSpec as P

F32 = jnp.float32
COARSE = 8
LOW_BOUND = 0.3
HIGH_BOUND = 2.0
COARSE_LOW = 0.02
VMEM_LIMIT = 28 * 1024 * 1024

SHAPE0, SHAPE1, SHAPE2, WINDOW_UNROLL = (1, True), (4, True), (4, True), True

SHAPE_K = (1, 5)

WINDOW = 23

PIECES = 4

KX, BX, KY, BY = 7, 6, 13, 12
PACKED_K = ((0, 9), (9, 9), (18, 4))
PACKED_B = ((0, 10), (10, 10))


def pairs(size, offset):
    found = []
    for i in range(offset, size - 1, 2):
        found += [(i, i + 1), (i + 1, i)]
    return found


def swap(value, axis, offset):
    return lax.ppermute(value, axis, pairs(lax.axis_size(axis), offset))


def chebyshev(sweeps, lower):
    middle = (HIGH_BOUND + lower) / 2
    half_width = (HIGH_BOUND - lower) / 2
    ratio = middle / half_width
    rho = 1 / ratio
    steps = []
    for _ in range(sweeps - 1):
        rho_next = 1 / (2 * ratio - rho)
        steps.append((rho_next * rho, 2 * rho_next / half_width))
        rho = rho_next
    return middle, steps


def iota(shape, axis):
    return lax.broadcasted_iota(jnp.int32, shape, axis)


def dot(a, b):
    b = b.astype(jnp.bfloat16)
    total = None
    for _ in range(3):
        piece = a.astype(jnp.bfloat16)
        a = a - piece.astype(F32)
        part = jnp.dot(piece, b, preferred_element_type=F32)
        total = part if total is None else total + part
    return total


def coarsen_matrix(fine, coarse, right, left, scale):
    f, c = iota((fine, coarse), 0), iota((fine, coarse), 1)
    ahead = (f < right) & (c == lax.shift_right_logical(f, 1))
    behind = (f >= fine - left) & (coarse - c == lax.shift_right_logical(fine - f + 1, 1))
    return jnp.where(ahead | behind, scale, 0.0).astype(F32)


def refine_matrix(coarse, fine, right, left):
    c, f = iota((coarse, fine), 0), iota((coarse, fine), 1)
    ahead = (f < right) & (c == lax.shift_right_logical(f, 1))
    behind = (f >= fine - left) & (coarse - c == lax.shift_right_logical(fine - f + 1, 1))
    return jnp.where(ahead | behind, 1.0, 0.0).astype(F32)


def turn(value, shift, axis):
    shift = shift % value.shape[axis]
    return value if shift == 0 else pltpu.roll(value, shift, axis=axis)


def edged(value, axis, top):
    depth = value.shape[axis]
    cut = functools.partial(lax.slice_in_dim, value, axis=axis)
    index = iota(value.shape[:axis] + (8,) + value.shape[axis + 1 :], axis)
    if top:
        edge = jnp.where(index == 7, 0.0, cut(depth - 8, depth))
        return edge if depth == 8 else jnp.concatenate([cut(0, depth - 8), edge], axis=axis)
    edge = jnp.where(index == 0, 0.0, cut(0, 8))
    return edge if depth == 8 else jnp.concatenate([edge, cut(8, depth)], axis=axis)


def weights_row(kc, km, kp, factor):
    axis = kc.ndim - 2
    up = kc + edged(turn(kc, -1, axis), axis, True)
    down = kc + edged(turn(kc, 1, axis), axis, False)
    ahead = kc + turn(kc, -1, axis + 1)
    behind = kc + turn(kc, 1, axis + 1)
    right = kc + kp
    left = kc + km
    diagonal = (up + down) + (ahead + behind) + (right + left)
    inverse = jnp.where(kc > 0, 1.0 / diagonal, 0.0)
    weights = [w * inverse for w in (left, right, behind, ahead, edged(down, axis, False), edged(up, axis, True))]
    return weights, inverse * (2.0 / factor), diagonal * (0.5 * factor)


def neighbour_sum(weights, below, centre, above):
    axis = centre.ndim - 2
    left, right, behind, ahead, down, up = weights
    total = left * below + right * above
    total = total + behind * turn(centre, 1, axis + 1) + ahead * turn(centre, -1, axis + 1)
    return total + down * turn(centre, 1, axis) + up * turn(centre, -1, axis)


def rows(low, high, body, chunk, unroll):
    full = (high - low) // chunk

    def step(n, carry):
        body(pl.ds(low + n * chunk, chunk), pl.ds(low + n * chunk - 1, chunk), pl.ds(low + n * chunk + 1, chunk))
        return carry

    lax.fori_loop(0, full, step, 0, unroll=unroll)
    at = low + full * chunk
    if at < high:
        body(pl.ds(at, high - at), pl.ds(at - 1, high - at), pl.ds(at + 1, high - at))


class Level:
    def __init__(self, k, weights, bh, x, p, factor, chunk, unroll):
        self.k, self.weights, self.bh, self.x, self.p, self.factor = k, weights, bh, x, p, factor
        self.chunk, self.unroll = chunk, unroll

    def rows(self, low, high, body):
        rows(low, high, body, self.chunk, self.unroll)

    def set_up(self, low, high, b=None, diagonal=None, inverses=None):
        def body(q, below, above):
            weights, inverse, diag = weights_row(self.k[q], self.k[below], self.k[above], self.factor)
            for n in range(6):
                self.weights[n, q] = weights[n]
            if b is not None:
                self.bh[q] = b[q] * inverse
            if inverses is not None:
                inverses[q] = inverse
            if diagonal is not None:
                diagonal[q] = diag

        self.rows(low, high, body)

    def total(self, x, q, below, above):
        return neighbour_sum([self.weights[n, q] for n in range(6)], x[below], x[q], x[above])

    def pre(self, low, high):
        middle, ((c1, c2),) = chebyshev(2, LOW_BOUND)

        def body(q, below, above):
            first = self.bh[q]
            total = self.total(self.bh, q, below, above)
            self.x[q] = (1 / middle) * (1 + c1 - c2 + c2 * middle) * first + (c2 / middle) * total

        self.rows(low, high, body)

    def residue(self, low, high, diagonal, out, at):
        def body(q, below, above):
            value = diagonal[q] * (self.bh[q] - self.x[q] + self.total(self.x, q, below, above))
            out[pl.ds(q.start + (at - low), q.size)] = value

        self.rows(low, high, body)

    def post(self, low, high, out):
        middle, ((c1, c2),) = chebyshev(2, LOW_BOUND)

        def first(q, below, above):
            update = (self.bh[q] - self.x[q] + self.total(self.x, q, below, above)) * (1 / middle)
            self.p[q] = update
            out[q] = self.x[q] + update

        def second(q, below, above):
            residue = self.bh[q] - out[q] + self.total(out, q, below, above)
            self.x[q] = out[q] + c1 * self.p[q] + c2 * residue

        self.rows(low - 1, high + 1, first)
        self.rows(low, high, second)


def spec(n):
    return [pl.BlockSpec(memory_space=pltpu.VMEM)] * n


def call(body, outs, scratch, *args, hbm_in=0, hbm_out=0, sems=(), cost=None):
    args = [pltpu.with_memory_space_constraint(x, pltpu.HBM) if n < hbm_in else x for n, x in enumerate(args)]
    return pl.pallas_call(
        body,
        out_shape=[pltpu.HBM(s, F32) if n < hbm_out else jax.ShapeDtypeStruct(s, F32) for n, s in enumerate(outs)],
        in_specs=[pl.BlockSpec(memory_space=pltpu.HBM)] * hbm_in + spec(len(args) - hbm_in),
        out_specs=[pl.BlockSpec(memory_space=pltpu.HBM)] * hbm_out + spec(len(outs) - hbm_out),
        scratch_shapes=[pltpu.VMEM(s, F32) for s in scratch] + [pltpu.SemaphoreType.DMA(s) for s in sems],
        compiler_params=pltpu.CompilerParams(vmem_limit_bytes=VMEM_LIMIT),
        cost_estimate=cost,
    )(*args)


class Copies:
    def __init__(self, sems):
        self.sems, self.used = sems, 0

    def start(self, source, target):
        copy = pltpu.make_async_copy(source, target, self.sems.at[self.used])
        copy.start()
        self.used += 1
        return copy


def odd(axis):
    return lax.rem(lax.axis_index(axis), 2) == 1


def pieces(n, source, target, copies):
    size = source.shape[0] // n
    return [copies.start(source.at[pl.ds(i * size, size)], target.at[pl.ds(i * size, size)]) for i in range(n)]


def strip_kernel(width, source, own, xa, xb, ref, sems):
    odd_x = odd("gx")
    depth = 64 // PIECES
    for n, copy in enumerate(pieces(PIECES, source, ref, Copies(sems))):
        copy.wait()
        z = pl.ds(depth * n, depth)
        planes = [ref[pl.ds(8 * depth * n + i, depth, stride=8), :] for i in range(8)]
        for i in range(8):
            own[i, z] = planes[i]
        for i in range(width):
            first, last = planes[i], planes[8 - width + i]
            xa[i, z] = jnp.where(odd_x, first, last)
            xb[i, z] = jnp.where(odd_x, last, first)


def pack_kernel(packed, width, own, xa, xb, rows_out, ya, yb):
    odd_x, odd_y = odd("gx"), odd("gy")
    lane = iota((64, 128), 1)
    halo = xa.shape[0]
    planes = [None] * (8 + 2 * halo)
    for n in range(halo):
        a, b = xa[n], xb[n]
        planes[n], planes[8 + halo + n] = jnp.where(odd_x, a, b), jnp.where(odd_x, b, a)
    for i in range(8):
        planes[halo + i] = own[i]
    for n, plane in enumerate(planes):
        rows_out[n] = plane
    for n, (start, count) in enumerate(packed):
        first, last = jnp.zeros((64, 128), F32), jnp.zeros((64, 128), F32)
        for i in range(count + 1):
            this, before = planes[start + min(i, count - 1)], planes[start + max(i - 1, 0)]
            turned = turn(jnp.where(lane < 64, this, before), width * i, 1)
            if i < count:
                first = jnp.where((lane >= width * i) & (lane < width * (i + 1)), turned, first)
            if i > 0:
                last = jnp.where((lane >= width * (i - 1)) & (lane < width * i), turned, last)
        ya[n] = jnp.where(odd_y, first, last)
        yb[n] = jnp.where(odd_y, last, first)


def outer_columns(packed, width, ya, yb):
    odd_y = odd("gy")
    lane = iota((64, 128), 1)
    for n, (start, count) in enumerate(packed):
        a, b = ya[n], yb[n]
        left, right = jnp.where(odd_y, a, b), jnp.where(odd_y, b, a)
        ahead = right
        for i in range(count):
            behind = turn(jnp.where(lane < width * (i + 1), left, right), -width * (i + 1), 1)
            yield start + i, jnp.where(lane < width, ahead, jnp.where(lane >= 128 - width, behind, 0.0))
            ahead = behind


def weights_kernel(
    k_rows, ya, yb, k_hbm, k1_hbm, weights, inverse, diagonal, k1, w1, inverse1, diagonal1, k_out, wide, thin, sems,
):
    copies = Copies(sems)
    for q, outer in outer_columns(PACKED_K, KY, ya, yb):
        k_out[q, :, 0:128] = k_rows[q]
        k_out[q, :, 128:256] = outer
    for m in range(10):
        wide[m] = k_out[2 * m + 1] + k_out[2 * m + 2]
    thin[...] = dot(wide[...].reshape(10 * 64, 256), coarsen_matrix(256, 128, 140, 12, 0.125))
    for m in range(10):
        k1[m] = thin[pl.ds(64 * m, 32, stride=2), :] + thin[pl.ds(64 * m + 1, 32, stride=2), :]
    flying = [copies.start(k_out.at[pl.ds(4, 14)], k_hbm), copies.start(k1, k1_hbm)]
    Level(k_out, weights, None, None, None, 1.0, *SHAPE_K).set_up(1, 21, None, diagonal, inverse)
    Level(k1, w1, None, None, None, 0.25, *SHAPE1).set_up(1, 9, None, diagonal1, inverse1)
    for copy in flying:
        copy.wait()


def first_kernel(
    count, b_rows, ya, yb, weights, inverse, diagonal, k1, w1, inverse1, diagonal1,
    bh_hbm, x_hbm, b1_hbm, x1_hbm, sa_hbm, sb_hbm, g_hbm,
    bh, x_out, b1, bh1, x1, sa, sb, fine, wide, thin, fine1, thin1, g_out, sems,
):
    odd_x = odd("gx")
    copies = Copies(sems)
    for n, outer in outer_columns(PACKED_B, BY, ya, yb):
        q = n + 1
        bh[q, :, 0:128] = b_rows[n] * inverse[q, :, 0:128]
        bh[q, :, 128:256] = outer * inverse[q, :, 128:256]
    flying = []
    level = Level(None, weights, bh, x_out, None, 1.0, *SHAPE0)
    level.pre(2, 20)
    level.residue(3, 19, diagonal, fine, 0)
    for m in range(8):
        wide[m] = fine[2 * m] + fine[2 * m + 1]
    thin[...] = dot(wide[...].reshape(8 * 64, 256), coarsen_matrix(256, 128, 140, 12, 0.125))
    for m in range(8):
        b1[1 + m] = thin[pl.ds(64 * m, 32, stride=2), :] + thin[pl.ds(64 * m + 1, 32, stride=2), :]
        bh1[1 + m] = b1[1 + m] * inverse1[1 + m]
    flying.append(copies.start(bh.at[pl.ds(5, 12)], bh_hbm))
    flying.append(copies.start(x_out.at[pl.ds(4, 14)], x_hbm))
    flying.append(copies.start(b1, b1_hbm))

    level = Level(None, w1, bh1, x1, None, 0.25, *SHAPE1)
    level.pre(2, 8)
    taken = ((x1, 3, 4), (x1, 4, 5), (x1, 5, 6), (b1, 4, 5), (k1, 3, 6))
    pack_outer([jnp.where(odd_x, ref[to_left], ref[to_right]) for ref, to_right, to_left in taken], sa)
    pack_outer([jnp.where(odd_x, ref[to_right], ref[to_left]) for ref, to_right, to_left in taken], sb)
    level.residue(3, 7, diagonal1, fine1, 0)
    parts = [fine1[0] + fine1[1], fine1[2] + fine1[3], k1[3] + k1[4], k1[5] + k1[6]]
    thin1[...] = dot(jnp.concatenate(parts, axis=0), coarsen_matrix(128, 128, 64, 0, 0.125))
    payload = jnp.zeros((16, 128), F32)
    for n in range(4):
        part = thin1[pl.ds(32 * n, 16, stride=2), :] + thin1[pl.ds(32 * n + 1, 16, stride=2), :]
        payload = payload + turn(part, 32 * n, 1)
    for n in range(count):
        g_out[n] = payload
    flying += pieces(PIECES, g_out, g_hbm, copies)
    flying += [copies.start(*pair) for pair in ((x1, x1_hbm), (sa, sa_hbm), (sb, sb_hbm))]
    for copy in flying:
        copy.wait()


def pack_outer(rows_in, out):
    lane = iota((32, 128), 1)
    out[0] = jnp.where(lane < 64, rows_in[0], turn(rows_in[1], 64, 1))
    out[1] = jnp.where(lane < 64, rows_in[2], turn(rows_in[3], 64, 1))
    last = rows_in[4]
    for n, row in enumerate(rows_in):
        at = 64 + 12 * n
        last = jnp.where((lane >= at) & (lane < at + 6), turn(row, 12 * n, 1), last)
        last = jnp.where((lane >= at + 6) & (lane < at + 12), turn(row, 12 * n - 52, 1), last)
    out[2] = last


def unpack_outer(tiles, n):
    lane = iota((32, 128), 1)
    own = turn(tiles[n // 2], 64 * (n % 2), 1)
    right, left = turn(tiles[2], -12 * n, 1), turn(tiles[2], 52 - 12 * n, 1)
    return jnp.where(lane < 64, own, jnp.where(lane < 70, right, jnp.where(lane >= 122, left, 0.0)))


def prepare_kernel(
    ra_hbm, rb_hbm, k1_hbm, b1_hbm, x1_hbm, k_hbm, bh_hbm, x_hbm, w0, bh0, d0, x0, w1, bh1, x1,
    ra, rb, k1_in, b1_in, x1_in, k0, k1, b1, sems,
):
    odd_x = odd("gx")
    copies = Copies(sems)
    for_level0 = [copies.start(k_hbm, k0), copies.start(bh_hbm, bh0.at[pl.ds(1, 12)]), copies.start(x_hbm, x0)]
    for_level1 = [copies.start(*pair) for pair in ((ra_hbm, ra), (rb_hbm, rb), (k1_hbm, k1_in), (b1_hbm, b1_in), (x1_hbm, x1_in))]
    for copy in for_level1:
        copy.wait()
    for side in range(2):
        tiles = [jnp.where(odd_x, ra[n], rb[n]) if side == 0 else jnp.where(odd_x, rb[n], ra[n]) for n in range(3)]
        for n in range(3):
            x1[n if side == 0 else 9 + n] = unpack_outer(tiles, n)
        b1[1 if side == 0 else 10] = unpack_outer(tiles, 3)
        k1[0 if side == 0 else 11] = unpack_outer(tiles, 4)
    for n in range(6):
        x1[3 + n] = x1_in[2 + n]
    for n in range(8):
        b1[2 + n] = b1_in[1 + n]
    for n in range(10):
        k1[1 + n] = k1_in[n]
    Level(k1, w1, bh1, None, None, 0.25, *SHAPE1).set_up(1, 11, b1)
    for copy in for_level0:
        copy.wait()
    Level(k0, w0, None, None, None, 1.0, *SHAPE0).set_up(1, 13, None, d0)


def window_start(me, count, window):
    return jnp.clip(me - WINDOW // 2, 0, count - window)


def last_kernel(
    count, w0, bh0, d0, x0, w1, bh1, x1, g, ga, gb, pressure, residual,
    k2, b2, w2, bh2, x2, y2, p2, fine2, sums2, coarse2, t1, y1, p1, stack1, t0, y0, p0, stack0, pressure_rows, residual_rows, sems,
):
    copies = Copies(sems)
    odd_y = odd("gy")
    me = lax.axis_index("gx")
    lane = iota((16, 128), 1)

    start = window_start(me, count, g.shape[0])

    def window(j, carry):
        device = me - WINDOW // 2 + j
        inside = (device >= 0) & (device < count)
        at = jnp.clip(device - start, 0, g.shape[0] - 1)
        own, a, b = g[at], ga[at], gb[at]
        left, right = jnp.where(odd_y, a, b), jnp.where(odd_y, b, a)
        by32 = turn(jnp.where(lane < 32, left, jnp.where(lane < 64, own, right)), -32, 1)
        by64 = turn(jnp.where(lane < 64, left, jnp.where(lane < 96, own, right)), -64, 1)
        by96 = turn(jnp.where(lane < 32, right, jnp.where(lane < 96, left, own)), -96, 1)
        for out, m, parts in ((b2, 0, (own, by96, by32)), (b2, 1, (by32, right, by64)), (k2, 0, (by64, by32, by96)), (k2, 1, (by96, by64, left))):
            value = jnp.where(lane < 32, parts[0], jnp.where(lane < 64, parts[1], jnp.where(lane >= 96, parts[2], 0.0)))
            out[2 * j + m] = jnp.where(inside, value, 0.0) if out is k2 else value
        return carry

    lax.fori_loop(0, WINDOW, window, 0, unroll=WINDOW_UNROLL)
    level = Level(k2, w2, bh2, x2, p2, 0.0625, *SHAPE2)
    level.set_up(1, 45, b2, y2)
    level.pre(2, 44)
    level.residue(4, 42, y2, fine2, 4)
    zero = jnp.zeros((16, 128), F32)
    for m in (0, 1, 21, 22):
        sums2[m] = zero
    for m in range(2, 21):
        sums2[m] = fine2[2 * m] + fine2[2 * m + 1]
    for m in range(23):
        sums2[23 + m] = k2[2 * m] + k2[2 * m + 1]
    coarse2[...] = dot(sums2[...].reshape(46 * 16, 128), coarsen_matrix(128, 128, 64, 32, 0.125))
    both = coarse2[pl.ds(0, 46 * 8, stride=2), :] + coarse2[pl.ds(1, 46 * 8, stride=2), :]
    both = both.reshape(46, 8, 128)
    b3, k3 = both[:23], both[23:]
    w3, inverse, _ = weights_row(k3[2:21], k3[1:20], k3[3:22], 0.015625)
    middle, steps = chebyshev(COARSE, COARSE_LOW)
    source = b3[2:21] * inverse
    update = source * (1 / middle)
    e3 = update
    for n, (c1, c2) in enumerate(steps):
        inner = slice(n + 1, 18 - n)
        below, centre, above = e3[:-2], e3[1:-1], e3[2:]
        total = neighbour_sum([w[inner] for w in w3], below, centre, above)
        update = c1 * update[1:-1] + c2 * (source[inner] - centre + total)
        e3 = centre + update

    tall = coarse2
    for m in range(5):
        for half in range(2):
            tall[pl.ds(16 * m + half, 8, stride=2), :] = e3[m]
    fine = dot(tall[0 : 5 * 16, :], refine_matrix(128, 128, 64, 32))
    for m in range(10):
        part = fine[16 * (m // 2) : 16 * (m // 2) + 16]
        x2[18 + m] = x2[18 + m] + part
    level.post(20, 26, y2)

    for m in range(6):
        for half in range(2):
            stack1[pl.ds(32 * m + half, 16, stride=2), :] = x2[20 + m]
    fine = dot(stack1[...], refine_matrix(128, 128, 70, 6))
    for m in range(12):
        t1[m] = x1[m] + fine[32 * (m // 2) : 32 * (m // 2) + 32]
    level = Level(None, w1, bh1, t1, p1, 0.25, *SHAPE1)
    level.post(2, 10, y1)

    for m in range(8):
        for half in range(2):
            stack0[pl.ds(64 * m + half, 32, stride=2), :] = t1[2 + m]
    matrix = refine_matrix(128, 256, 140, 12)
    fine = dot(stack0[...], matrix)
    for m in range(14):
        row = (m + 1) // 2
        t0[m] = x0[m] + fine[64 * row : 64 * row + 64]
    level = Level(None, w0, bh0, t0, p0, 1.0, *SHAPE0)
    level.post(2, 12, y0)
    for i in range(8):
        pressure_rows[pl.ds(i, 64, stride=8), :] = t0[3 + i, :, 0:128]
    waits = pieces(PIECES, pressure_rows, pressure, copies)
    for i in range(8):
        q = 3 + i
        value = d0[q] * (bh0[q] - t0[q] + level.total(t0, q, q - 1, q + 1))
        residual_rows[pl.ds(i, 64, stride=8), :] = value[:, 0:128]
    waits += pieces(PIECES, residual_rows, residual, copies)
    for copy in waits:
        copy.wait()


def on_device(right_side, conductivity):
    count = lax.axis_size("gx")
    b, k = right_side.reshape(512, 128), conductivity.reshape(512, 128)
    plane = (64, 128)

    def strips(value, width):
        own, xa, xb = call(
            functools.partial(strip_kernel, width),
            [(8,) + plane] + [(width,) + plane] * 2,
            [(512, 128)],
            value,
            hbm_in=1,
            sems=[(PIECES,)],
        )
        return own, swap(xa, "gx", 0), swap(xb, "gx", 1)

    own_k, xka, xkb = strips(k, KX)
    own_b, xba, xbb = strips(b, BX)

    def packed(own, xa, xb, pack, width):
        rows_out, ya, yb = call(
            functools.partial(pack_kernel, pack, width),
            [(8 + 2 * xa.shape[0],) + plane] + [(len(pack),) + plane] * 2,
            [],
            own, xa, xb,
            cost=pl.CostEstimate(flops=1_000_000, bytes_accessed=2_000_000, transcendentals=0),
        )
        return rows_out, swap(ya, "gy", 0), swap(yb, "gy", 1)

    rows0, rows1, rows2, rows3 = (22, 64, 256), (10, 32, 128), (46, 16, 128), (12, 32, 128)
    wide0 = (14, 64, 256)
    k0, k1, *about_k = call(
        weights_kernel,
        [wide0, rows1, (6,) + rows0, rows0, rows0, rows1, (6,) + rows1, rows1, rows1],
        [rows0, (10, 64, 256), (10 * 64, 128)],
        *packed(own_k, xka, xkb, PACKED_K, KY),
        hbm_out=2,
        sems=[(2,)],
        cost=pl.CostEstimate(flops=20_000_000, bytes_accessed=8_000_000, transcendentals=300_000),
    )
    bh0, x0, b1, x1, sa, sb, g = call(
        functools.partial(first_kernel, count),
        [(12, 64, 256), wide0, rows1, rows1, (3, 32, 128), (3, 32, 128), (count, 16, 128)],
        [rows0, rows0, rows1, rows1, rows1, (3, 32, 128), (3, 32, 128)]
        + [(16, 64, 256), (8, 64, 256), (8 * 64, 128), (4, 32, 128), (128, 128), (count, 16, 128)],
        *packed(own_b, xba, xbb, PACKED_B, BY), *about_k,
        hbm_out=7,
        sems=[(6 + PIECES,)],
    )
    ra, rb = swap(sa, "gx", 0), swap(sb, "gx", 1)
    g = lax.all_to_all(g, "gx", 0, 0, tiled=True)
    g, ra, rb, k0, bh0, x0, k1, b1, x1 = lax.optimization_barrier((g, ra, rb, k0, bh0, x0, k1, b1, x1))
    window = min(WINDOW, count)
    g = lax.dynamic_slice_in_dim(g, window_start(lax.axis_index("gx"), count, window), window)
    ga, gb = swap(g, "gy", 0), swap(g, "gy", 1)
    kept = call(
        prepare_kernel,
        [(6,) + wide0, wide0, wide0, wide0, (6,) + rows3, rows3, rows3],
        [(3, 32, 128), (3, 32, 128), rows1, rows1, rows1, wide0, rows3, rows3],
        ra, rb, k1, b1, x1, k0, bh0, x0,
        hbm_in=8,
        sems=[(8,)],
        cost=pl.CostEstimate(flops=20_000_000, bytes_accessed=8_000_000, transcendentals=200_000),
    )
    pressure, residual = call(
        functools.partial(last_kernel, count),
        [(512, 128)] * 2,
        [rows2, rows2, (6,) + rows2, rows2, rows2, rows2, rows2, rows2, rows2, (46 * 16, 128)]
        + [rows3, rows3, rows3, (6 * 32, 128)]
        + [wide0, wide0, wide0, (8 * 64, 128), (512, 128), (512, 128)],
        *kept, g, ga, gb,
        hbm_out=2,
        sems=[(2 * PIECES,)],
    )
    return pressure.reshape(64, 8, 128), residual.reshape(64, 8, 128)


def solution(mesh):
    place = P(None, "gx", "gy")
    return jax.shard_map(
        on_device, mesh=mesh, in_specs=(place, place), out_specs=(place, place), check_vma=False
    )
```
